32 devices in a mesh: dp: 4 (over x, core), ctx: 2 (over y), tensor: 4 (over z).
Axes of the slice: x: 2, y: 2, z: 4, core: 2. Of those that a mesh axis runs over, the one named last changes fastest.
Arguments:
- layer_input: bfloat16 [4, 1536, 2560], P('dp', 'ctx'), may hold values from -6 to 6
- cotangent: bfloat16 [4, 1536, 2560], P('dp', 'ctx'), may hold values from -6 to 6
- span_order: int32 [4], replicated, may hold values from 0 to 3, each once
- query_down: bfloat16 [2560, 768], P(('dp', 'ctx')), may hold values from -0.125 to 0.125
- latent_down: bfloat16 [2560, 288], P(('dp', 'ctx')), may hold values from -0.125 to 0.125
- query_up: bfloat16 [768, 3840], P(('dp', 'ctx'), 'tensor'), may hold values from -0.21875 to 0.21875
- latent_up: bfloat16 [256, 5120], P(('dp', 'ctx'), 'tensor'), may hold values from -0.375 to 0.375
- output_weight: bfloat16 [2560, 2560], P('tensor', ('dp', 'ctx')), may hold values from -4 to 4
- gate_weight: bfloat16 [2560, 6400], P(('dp', 'ctx'), 'tensor'), may hold values from -0.125 to 0.125
- up_weight: bfloat16 [2560, 6400], P(('dp', 'ctx'), 'tensor'), may hold values from -0.125 to 0.125
- down_weight: bfloat16 [6400, 2560], P('tensor', ('dp', 'ctx')), may hold values from -0.625 to 0.625
- first_gain: float32 [2560], replicated, may hold values from 0.25 to 1.75
- query_gain: float32 [768], replicated, may hold values from 0.25 to 1.75
- latent_gain: float32 [256], replicated, may hold values from 0.25 to 1.75
- second_gain: float32 [2560], replicated, may hold values from 0.25 to 1.75
Outputs:
- block_out: bfloat16 [4, 1536, 2560], P('dp', 'ctx')
- input_grad: float32 [4, 1536, 2560], P('dp', 'ctx')
- query_down_grad: float32 [2560, 768], P(('dp', 'ctx'), 'tensor')
- latent_down_grad: float32 [2560, 288], P(('dp', 'ctx'), 'tensor')
- query_up_grad: float32 [768, 3840], P(('dp', 'ctx'), 'tensor')
- latent_up_grad: float32 [256, 5120], P(('dp', 'ctx'), 'tensor')
- output_grad: float32 [2560, 2560], P('tensor', ('dp', 'ctx'))
- gate_grad: float32 [2560, 6400], P(('dp', 'ctx'), 'tensor')
- up_grad: float32 [2560, 6400], P(('dp', 'ctx'), 'tensor')
- down_grad: float32 [6400, 2560], P('tensor', ('dp', 'ctx'))
- first_gain_grad: float32 [2560], P(('dp', 'ctx'))
- query_gain_grad: float32 [768], P(('dp', 'ctx'))
- latent_gain_grad: float32 [256], P(('dp', 'ctx'))
- second_gain_grad: float32 [2560], P(('dp', 'ctx'))
The draws below stay inside these ranges and needn't reach their ends.
Inputs may be any that keep to these rules, and one draw needn't show every extreme that they name: A permutation: stored block b of every sequence (384 tokens; a device of ctx holds two neighbouring stored blocks) holds positions span_order[b] * 384 onward.
All inputs are finite; a program needn't handle non-finite values.
Results may differ from the reference program's by a relative error of at most 0.025.
Values may be sent and summed in bfloat16 or wider, within the bound.
No kernel may reach another device: no remote copies, remote signals or barrier semaphores. Data moves between devices by JAX's collectives and lax.ppermute only.
A program may use at most 256 MiB of HBM per device.

```python
import math
import jax
import jax.numpy as jnp
from jax import lax

D = 2560
HEADS = 40
NOPE = 64
ROPE = 32
VDIM = 64
QRANK = 768
KVRANK = 256
FF = 6400
SEQS = 4
LENGTH = 1536
SPAN = 384
N_CTX = 2


def raised(values, stream_key, source, target, shards_of, factor):
    def block_of(axis_at):
        return (jnp.arange(values.shape[axis_at]) // (values.shape[axis_at] // shards_of)).reshape((-1,) + (1,) * (values.ndim - 1 - axis_at))

    first = jax.random.permutation(stream_key, shards_of)[block_of(target)]
    other_side = (block_of(target) + shards_of // 2) % shards_of
    return jnp.where((block_of(source) == first) | (block_of(source) == other_side), factor * values, values)


def level_of(stream_key, extent, split, low, high):
    def one(axis_at, blocks):
        steps = jax.random.uniform(jax.random.fold_in(jax.random.fold_in(stream_key, 6), axis_at), (blocks,), jnp.float32, low / len(split), high / len(split))
        return jnp.repeat(jnp.exp(steps), extent[axis_at] // blocks).reshape((-1,) + (1,) * (len(extent) - axis_at - 1))

    factor_of = one(*split[0])
    for cut in split[1:]:
        factor_of = factor_of * one(*cut)
    return factor_of


def scatter_about(rng, extent, scale, most, cuts=(), held_as=jnp.bfloat16):
    array = jax.random.normal(rng, extent, jnp.float32) * scale
    if len(cuts) > 0:
        array = level_of(rng, extent, cuts, -0.22, 0.18) * array
    return jnp.clip(array, min=-most, max=most).astype(held_as)


def gaussian_with(stream_key, shape, spread, most, cuts, heavy, kind=jnp.bfloat16):
    array = spread * jax.random.normal(stream_key, shape, jnp.float32)
    if cuts:
        array = array * level_of(stream_key, shape, cuts, -0.22, 0.18)
    return jnp.clip(raised(array, jax.random.fold_in(stream_key, 3), *heavy), -most, most).astype(kind)


def setup_inputs(seed: int = 0) -> dict:
    splits = jax.random.split(jax.random.key(seed), 16)
    layer_input = scatter_about(splits[0], (SEQS, LENGTH, D), 1.0, 6.0, ((0, 4), (1, 2)))
    cotangent = gaussian_with(splits[1], (SEQS, LENGTH, D), 1.0, 6.0, ((0, 4), (1, 2)), (0, 2, 4, 2.0))
    span_order = jax.random.permutation(splits[2], 2 * N_CTX).astype(jnp.int32)
    query_down = scatter_about(splits[3], (D, QRANK), D ** -0.5, 0.125, ((0, 8),))
    latent_down = scatter_about(splits[4], (D, KVRANK + ROPE), D ** -0.5, 0.125, ((0, 8),))
    query_up = scatter_about(splits[5], (QRANK, HEADS * (NOPE + ROPE)), QRANK ** -0.5, 0.21875, ((0, 8), (1, 4)))
    latent_up = scatter_about(splits[6], (KVRANK, HEADS * (NOPE + VDIM)), KVRANK ** -0.5, 0.375, ((0, 8), (1, 4)))
    output_weight = scatter_about(splits[7], (HEADS * VDIM, D), (max(HEADS * VDIM // 1024, 1)) ** -0.5, 4.0, ((0, 4), (1, 8)))
    gate_weight = scatter_about(splits[8], (D, FF), D ** -0.5, 0.125, ((0, 8), (1, 4)))
    up_weight = scatter_about(splits[9], (D, FF), D ** -0.5, 0.125, ((0, 8), (1, 4)))
    down_weight = scatter_about(splits[10], (FF, D), (FF // 64) ** -0.5, 0.625, ((0, 4), (1, 8)))
    first_gain = jnp.clip(1.0 + 0.15 * jax.random.normal(splits[11], (D,), jnp.float32), 0.25, 1.75)
    query_gain = jnp.clip(1.0 + 0.15 * jax.random.normal(splits[12], (QRANK,), jnp.float32), 0.25, 1.75)
    latent_gain = jnp.clip(1.0 + 0.15 * jax.random.normal(splits[13], (KVRANK,), jnp.float32), 0.25, 1.75)
    second_gain = jnp.clip(1.0 + 0.15 * jax.random.normal(splits[14], (D,), jnp.float32), 0.25, 1.75)
    return {"layer_input": layer_input, "cotangent": cotangent, "span_order": span_order, "query_down": query_down, "latent_down": latent_down, "query_up": query_up, "latent_up": latent_up, "output_weight": output_weight, "gate_weight": gate_weight, "up_weight": up_weight, "down_weight": down_weight, "first_gain": first_gain, "query_gain": query_gain, "latent_gain": latent_gain, "second_gain": second_gain}


depth_scale = 1.4 / math.sqrt(62.0)
eps_value = 1e-05
masked_value = -1e+30

@jax.custom_vjp
def low(v):
    return lax.optimization_barrier(v.astype(jnp.bfloat16)).astype(jnp.float32)

@jax.custom_vjp
def low_back(v):
    return v

def low_keep(v):
    return (low(v), None)

def low_pass(kept, grad):
    return (grad,)

def back_keep(v):
    return (v, None)

def back_low(kept, grad):
    return (low(grad),)
low.defvjp(low_keep, low_pass)
low_back.defvjp(back_keep, back_low)

def matmul(left, right):
    return jnp.dot(left, right, precision=lax.Precision.HIGHEST, preferred_element_type=jnp.float32)

def rms_norm(values, gain):
    return values * lax.rsqrt(lax.optimization_barrier(jnp.mean(values * values, axis=-1, keepdims=True)) + eps_value) * gain

def positions(span_order, start_index, row_count, span_rows):
    index = start_index + jnp.arange(row_count, dtype=jnp.int32)
    blocks = index // span_rows
    matches = blocks[:, None] == jnp.arange(span_order.shape[0], dtype=jnp.int32)[None, :]
    span_start = lax.optimization_barrier(jnp.sum(jnp.where(matches, span_order[None, :], 0), axis=1)).astype(jnp.int32)
    return span_start * span_rows + index % span_rows

def angles(places, width):
    half_width = width // 2
    spectrum = 10000.0 ** (-2.0 * jnp.arange(half_width, dtype=jnp.float32) / width)
    turned = places.astype(jnp.float32)[:, None] * spectrum[None, :]
    return (jnp.cos(turned), jnp.sin(turned))

def rotate(values, cosine, sine):
    half_width = values.shape[-1] // 2
    former = values[..., :half_width]
    latter = values[..., half_width:]
    return jnp.concatenate([former * cosine - latter * sine, latter * cosine + former * sine], axis=-1)

def layer(inputs, params, places):
    query_down, latent_down, query_up, latent_up, output_weight, gate_weight, up_weight, down_weight, first_gain, query_gain, latent_gain, second_gain = params
    cosine, sine = angles(places, ROPE)
    norm_one = low(rms_norm(inputs, first_gain))
    query_latent = low_back(matmul(norm_one, query_down))
    query_normed = low(rms_norm(query_latent, query_gain))
    latent_raw = low_back(matmul(norm_one, latent_down))
    latent_normed = low(rms_norm(latent_raw[:, :KVRANK], latent_gain))
    rotary_key = low(rotate(latent_raw[:, KVRANK:], cosine, sine))
    query_raw = low_back(matmul(query_normed, query_up)).reshape(LENGTH, HEADS, NOPE + ROPE)
    queries = low(jnp.concatenate([query_raw[..., :NOPE], rotate(query_raw[..., NOPE:], cosine[:, None, :], sine[:, None, :])], axis=-1))
    key_value = low(low_back(matmul(latent_normed, latent_up))).reshape(LENGTH, HEADS, NOPE + VDIM)
    keys = jnp.concatenate([key_value[..., :NOPE], jnp.broadcast_to(rotary_key[:, None, :], (LENGTH, HEADS, ROPE))], axis=-1)
    values = key_value[..., NOPE:]
    visible = places[None, :] <= places[:, None]
    score_scale = 1.0 / math.sqrt(NOPE + ROPE)

    def attend(parts):
        query_head, key_head, value_head = parts
        scores = low_back(matmul(query_head, key_head.T) * score_scale)
        scores = jnp.where(visible, scores, masked_value)
        expo = jnp.exp(scores - lax.optimization_barrier(jnp.max(scores, axis=1, keepdims=True)))
        weights = low(expo / lax.optimization_barrier(jnp.sum(expo, axis=1, keepdims=True)))
        return matmul(weights, value_head)
    heads_out = lax.map(jax.checkpoint(attend), (jnp.transpose(queries, (1, 0, 2)), jnp.transpose(keys, (1, 0, 2)), jnp.transpose(values, (1, 0, 2))))
    attended = low_back(low(jnp.transpose(heads_out, (1, 0, 2)).reshape(LENGTH, HEADS * VDIM)))
    attn_term = low_back(matmul(attended, output_weight))
    middle = inputs + depth_scale * attn_term
    norm_two = low(rms_norm(middle, second_gain))
    gate_value = low_back(matmul(norm_two, gate_weight))
    up_value = low_back(matmul(norm_two, up_weight))
    hidden = low(jax.nn.silu(gate_value) * up_value)
    ffn_term = low_back(matmul(hidden, down_weight))
    return middle + depth_scale * ffn_term

def reference(layer_input, cotangent, span_order, query_down, latent_down, query_up, latent_up, output_weight, gate_weight, up_weight, down_weight, first_gain, query_gain, latent_gain, second_gain):
    params = tuple((argument.astype(jnp.float32) for argument in (query_down, latent_down, query_up, latent_up, output_weight, gate_weight, up_weight, down_weight, first_gain, query_gain, latent_gain, second_gain)))
    places = positions(span_order, 0, LENGTH, SPAN)

    def one_sequence(totals, sequence_pair):
        seq_input, seq_cot = sequence_pair
        result, pullback = jax.vjp(lambda inputs, weights: layer(inputs, weights, places), seq_input.astype(jnp.float32), params)
        grad_input, weight_grads = pullback(seq_cot.astype(jnp.float32))
        totals = tuple((total + grad for total, grad in zip(totals, weight_grads)))
        return (totals, (result.astype(jnp.bfloat16), grad_input))
    start_totals = tuple((jnp.zeros(argument.shape, jnp.float32) for argument in params))
    totals, (block_out, input_grad) = lax.scan(one_sequence, start_totals, (layer_input, cotangent))
    return (block_out, input_grad) + totals
```

```python
import math

import jax
import jax.numpy as jnp
from jax import lax
from jax.experimental import pallas as pl
from jax.experimental.pallas import tpu as pltpu
from jax.sharding import PartitionSpec as P

NOPE = 64
ROPE = 32
VDIM = 64
QRANK = 768
KVRANK = 256
HEAD = NOPE + ROPE
PAIR = NOPE + VDIM

depth_scale = 1.4 / math.sqrt(62.0)
eps_value = 1e-05
masked_value = -1e30
score_scale = 1.0 / math.sqrt(NOPE + ROPE)
log2_scale = score_scale / math.log(2.0)

f32 = jnp.float32
bf16 = jnp.bfloat16


def contract(left, right, left_dim, right_dim):
    return lax.dot_general(
        left, right, (((left_dim,), (right_dim,)), ((), ())), preferred_element_type=f32
    )


def rms_norm(values, gain, axis=0):
    factor = lax.rsqrt(jnp.mean(values * values, axis=axis, keepdims=True) + eps_value)
    gain = gain[:, None] if axis == 0 else gain
    return (values * factor * gain, factor)


def rms_back(grad_out, values, factor, gain, axis=0):
    normed = values * factor
    scaled = grad_out * (gain[:, None] if axis == 0 else gain)
    grad_in = factor * (scaled - normed * jnp.mean(scaled * normed, axis=axis, keepdims=True))
    return (grad_in, jnp.sum(grad_out * normed, axis=axis + 1))


def angles(places, width):
    half_width = width // 2
    spectrum = 10000.0 ** (-2.0 * jnp.arange(half_width, dtype=jnp.float32) / width)
    turned = spectrum[:, None] * places.astype(jnp.float32)[None, :]
    return (jnp.cos(turned), jnp.sin(turned))


def rotate(values, cosine, sine):
    half = values.shape[0] // 2
    former, latter = values[:half], values[half:]
    return jnp.concatenate(
        [former * cosine - latter * sine, latter * cosine + former * sine], axis=0
    )


def unrotate(values, cosine, sine):
    half = values.shape[0] // 2
    former, latter = values[:half], values[half:]
    return jnp.concatenate(
        [former * cosine + latter * sine, latter * cosine - former * sine], axis=0
    )


def joined_keys(pairs, rotary):
    lane = lax.broadcasted_iota(jnp.int32, pairs.shape, 1)
    return jnp.where(lane < NOPE, pairs, rotary)


def attend_kernel(blocks, span, own, places, query_raw, cosine, sine, pairs, rotary, out, query_out, log_out, top, total, acc):
    half = ROPE // 2
    former = query_raw[NOPE : NOPE + half, :]
    latter = query_raw[NOPE + half :, :]
    query = jnp.concatenate(
        [
            query_raw[:NOPE, :],
            former * cosine[...] - latter * sine[...],
            latter * cosine[...] + former * sine[...],
        ],
        axis=0,
    ).astype(bf16)
    query_out[...] = query
    top[...] = jnp.full(top.shape, masked_value, f32)
    total[...] = jnp.zeros(total.shape, f32)
    acc[...] = jnp.zeros(acc.shape, f32)
    mine = places[own]

    def visit(block, diagonal):
        rows = pl.ds(block * span, span)
        pair = pairs[rows, :]
        key = joined_keys(pair, rotary[rows, :])[:, :HEAD]
        scores = contract(key, query, 1, 0)
        if diagonal:
            key_at = lax.broadcasted_iota(jnp.int32, scores.shape, 0)
            query_at = lax.broadcasted_iota(jnp.int32, scores.shape, 1)
            scores = jnp.where(key_at <= query_at, scores, masked_value)
        before = top[...]
        highest = jnp.maximum(before, jnp.max(scores, axis=0, keepdims=True))
        expo = jnp.exp2((scores - highest) * log2_scale)
        shrink = jnp.exp2((before - highest) * log2_scale)
        top[...] = highest
        total[...] = total[...] * shrink + jnp.sum(expo, axis=0, keepdims=True)
        acc[...] = acc[...] * shrink + contract(pair, expo.astype(bf16), 0, 0)

    for block in range(blocks):
        theirs = places[block]
        pl.when(theirs < mine)(lambda block=block: visit(block, False))
        pl.when(theirs == mine)(lambda block=block: visit(block, True))
    out[...] = (acc[NOPE:, :] / total[...]).astype(bf16)
    log_out[0] = top[...] * log2_scale + jnp.log2(total[...])


def attend(own, places, query_raw, cosine, sine, pairs, rotary):
    rows, tokens = query_raw.shape
    heads = rows // HEAD
    keys = pairs.shape[0]
    span = tokens
    blocks = keys // span
    elements = heads * tokens * keys
    half = ROPE // 2

    def kernel(*refs):
        attend_kernel(blocks, span, own, *refs)

    return pl.pallas_call(
        kernel,
        out_shape=(
            jax.ShapeDtypeStruct((heads * VDIM, tokens), bf16),
            jax.ShapeDtypeStruct((rows, tokens), bf16),
            jax.ShapeDtypeStruct((heads, 1, tokens), f32),
        ),
        grid_spec=pltpu.PrefetchScalarGridSpec(
            num_scalar_prefetch=1,
            grid=(heads,),
            in_specs=[
                pl.BlockSpec((HEAD, tokens), lambda h, p: (h, 0)),
                pl.BlockSpec((half, tokens), lambda h, p: (0, 0)),
                pl.BlockSpec((half, tokens), lambda h, p: (0, 0)),
                pl.BlockSpec((keys, PAIR), lambda h, p: (0, h)),
                pl.BlockSpec((keys, PAIR), lambda h, p: (0, 0)),
            ],
            out_specs=(
                pl.BlockSpec((VDIM, tokens), lambda h, p: (h, 0)),
                pl.BlockSpec((HEAD, tokens), lambda h, p: (h, 0)),
                pl.BlockSpec((1, 1, tokens), lambda h, p: (h, 0, 0)),
            ),
            scratch_shapes=[
                pltpu.VMEM((1, tokens), f32),
                pltpu.VMEM((1, tokens), f32),
                pltpu.VMEM((PAIR, tokens), f32),
            ],
        ),
        compiler_params=pltpu.CompilerParams(vmem_limit_bytes=32 * 1024 * 1024),
        cost_estimate=pl.CostEstimate(
            flops=4 * elements * 128, bytes_accessed=keys * heads * PAIR * 2, transcendentals=elements
        ),
        name="attend",
    )(places, query_raw, cosine, sine, pairs, rotary)


def attend_back_kernel(blocks, span, start, own, places, query_in, cosine, sine, pairs, rotary, grad_in, out_in, log_in, *rest):
    if start:
        base, query_grad, pair_grad, rotary_grad, acc = rest
    else:
        query_grad, pair_grad, rotary_grad, acc = rest
    half = ROPE // 2
    mine = places[own]
    query = query_in[...]
    grad = grad_in[...]
    inner = jnp.sum(grad.astype(f32) * out_in[...].astype(f32), axis=0, keepdims=True)
    grad_tall = jnp.concatenate([jnp.zeros((NOPE, grad.shape[1]), bf16), grad], axis=0)
    query_tall = jnp.concatenate([query, jnp.zeros((PAIR - HEAD, grad.shape[1]), bf16)], axis=0)
    log_total = log_in[0]
    acc[...] = jnp.zeros(acc.shape, f32)

    @pl.when(pl.program_id(0) == 0)
    def _():
        rotary_grad[...] = jnp.zeros(rotary_grad.shape, f32)

    def visit(block, diagonal):
        rows = pl.ds(block * span, span)
        pair = pairs[rows, :]
        key = joined_keys(pair, rotary[rows, :])
        scores = contract(key, query_tall, 1, 0)
        probs = jnp.exp2(scores * log2_scale - log_total)
        if diagonal:
            key_at = lax.broadcasted_iota(jnp.int32, scores.shape, 0)
            query_at = lax.broadcasted_iota(jnp.int32, scores.shape, 1)
            probs = jnp.where(key_at <= query_at, probs, 0.0)
        grad_probs = contract(pair, grad_tall, 1, 0)
        grad_scores = (probs * (grad_probs - inner)).astype(bf16)
        key_part = contract(grad_scores, query_tall, 1, 1) * score_scale
        value_part = contract(probs.astype(bf16), grad_tall, 1, 1)
        lane = lax.broadcasted_iota(jnp.int32, key_part.shape, 1)
        both = jnp.where(lane < NOPE, key_part, value_part)
        if start:
            both = both + base[rows, :].astype(f32)
        pair_grad[rows, :] = both.astype(bf16)
        rotary_grad[rows, :] += key_part
        acc[...] += contract(key, grad_scores, 0, 0)

    def skip(block):
        rows = pl.ds(block * span, span)
        if start:
            pair_grad[rows, :] = base[rows, :]
        else:
            pair_grad[rows, :] = jnp.zeros((span, PAIR), bf16)

    for block in range(blocks):
        theirs = places[block]
        pl.when(theirs < mine)(lambda block=block: visit(block, False))
        pl.when(theirs == mine)(lambda block=block: visit(block, True))
        pl.when(theirs > mine)(lambda block=block: skip(block))
    total = acc[...] * score_scale
    former = total[NOPE : NOPE + half, :]
    latter = total[NOPE + half : HEAD, :]
    query_grad[...] = jnp.concatenate(
        [
            total[:NOPE, :],
            former * cosine[...] + latter * sine[...],
            latter * cosine[...] - former * sine[...],
        ],
        axis=0,
    ).astype(bf16)


def attend_back(own, places, query, cosine, sine, pairs, rotary, grad, out, log_total, base):
    rows, tokens = query.shape
    heads = rows // HEAD
    keys = pairs.shape[0]
    span = tokens
    blocks = keys // span
    elements = heads * tokens * keys
    half = ROPE // 2
    start = base is not None

    def kernel(*refs):
        attend_back_kernel(blocks, span, start, own, *refs)

    args = [places, query, cosine, sine, pairs, rotary, grad, out, log_total]
    in_specs = [
        pl.BlockSpec((HEAD, tokens), lambda h, p: (h, 0)),
        pl.BlockSpec((half, tokens), lambda h, p: (0, 0)),
        pl.BlockSpec((half, tokens), lambda h, p: (0, 0)),
        pl.BlockSpec((keys, PAIR), lambda h, p: (0, h)),
        pl.BlockSpec((keys, PAIR), lambda h, p: (0, 0)),
        pl.BlockSpec((VDIM, tokens), lambda h, p: (h, 0)),
        pl.BlockSpec((VDIM, tokens), lambda h, p: (h, 0)),
        pl.BlockSpec((1, 1, tokens), lambda h, p: (h, 0, 0)),
    ]
    if start:
        args.append(base)
        in_specs.append(pl.BlockSpec((keys, PAIR), lambda h, p: (0, h)))
    return pl.pallas_call(
        kernel,
        out_shape=(
            jax.ShapeDtypeStruct((rows, tokens), bf16),
            jax.ShapeDtypeStruct((keys, heads * PAIR), bf16),
            jax.ShapeDtypeStruct((keys, PAIR), f32),
        ),
        grid_spec=pltpu.PrefetchScalarGridSpec(
            num_scalar_prefetch=1,
            grid=(heads,),
            in_specs=in_specs,
            out_specs=(
                pl.BlockSpec((HEAD, tokens), lambda h, p: (h, 0)),
                pl.BlockSpec((keys, PAIR), lambda h, p: (0, h)),
                pl.BlockSpec((keys, PAIR), lambda h, p: (0, 0)),
            ),
            scratch_shapes=[pltpu.VMEM((PAIR, tokens), f32)],
        ),
        compiler_params=pltpu.CompilerParams(vmem_limit_bytes=32 * 1024 * 1024),
        cost_estimate=pl.CostEstimate(
            flops=10 * elements * 128, bytes_accessed=keys * heads * PAIR * 4, transcendentals=elements
        ),
        name="attend_back",
    )(*args)


def ffn_front(normed, grad, weights, tile=256):
    tokens, width = normed.shape
    owners, kinds, rows, units = weights.shape

    def kernel(normed, grad, gate, up, down, hidden, grad_gate, grad_up):
        def product(left, weight):
            weight = weight[...].reshape(width, tile)
            return jnp.dot(left[...], weight, preferred_element_type=f32)

        gate_value = product(normed, gate)
        up_value = product(normed, up)
        grad_hidden = product(grad, down)
        sigma = jax.nn.sigmoid(gate_value)
        silu_gate = gate_value * sigma
        hidden[...] = (silu_gate * up_value).astype(bf16)
        slope = sigma * (1.0 + gate_value * (1.0 - sigma))
        grad_gate[...] = (grad_hidden * up_value * slope).astype(bf16)
        grad_up[...] = (grad_hidden * silu_gate).astype(bf16)

    whole = pl.BlockSpec((tokens, width), lambda n: (0, 0))
    weight = [
        pl.BlockSpec((owners, None, rows, tile), lambda n, kind=kind: (0, kind, 0, n))
        for kind in range(kinds)
    ]
    given = jax.ShapeDtypeStruct((tokens, units), bf16)
    block = pl.BlockSpec((tokens, tile), lambda n: (0, n))
    return pl.pallas_call(
        kernel,
        out_shape=(given, given, given),
        grid=(pl.cdiv(units, tile),),
        in_specs=[whole, whole] + weight,
        out_specs=(block, block, block),
        compiler_params=pltpu.CompilerParams(vmem_limit_bytes=40 * 1024 * 1024),
        cost_estimate=pl.CostEstimate(
            flops=6 * tokens * width * units,
            bytes_accessed=6 * width * units,
            transcendentals=tokens * units,
        ),
        name="ffn_front",
    )(normed, grad, weights, weights, weights)


def owners_at_once(rows):
    step = 1
    while step * rows % 128:
        step += 1
    return step


def rows_product(lefts, weights, kinds):
    tokens, units = lefts[0].shape
    owners, _, rows, _ = weights.shape
    step = owners_at_once(rows)
    tile = step * rows
    width = owners * rows
    count = len(lefts)

    def kernel(*refs):
        total = None
        for i in range(count):
            weight = refs[count + i][...].reshape(tile, units)
            part = contract(refs[i][...], weight, 1, 1)
            total = part if total is None else total + part
        refs[-1][...] = total.astype(bf16)

    whole = pl.BlockSpec((tokens, units), lambda n: (0, 0))
    weight = [
        pl.BlockSpec((step, None, rows, units), lambda n, kind=kind: (n, kind, 0, 0))
        for kind in kinds
    ]
    return pl.pallas_call(
        kernel,
        out_shape=jax.ShapeDtypeStruct((tokens, width), bf16),
        grid=(width // tile,),
        in_specs=[whole] * count + weight,
        out_specs=pl.BlockSpec((tokens, tile), lambda n: (0, n)),
        compiler_params=pltpu.CompilerParams(vmem_limit_bytes=40 * 1024 * 1024),
        cost_estimate=pl.CostEstimate(
            flops=2 * count * tokens * width * units,
            bytes_accessed=2 * count * width * units,
            transcendentals=0,
        ),
        name="rows_product",
    )(*lefts, *([weights] * count))


def weight_grads(lefts, rights, owners):
    tokens, width = lefts[0].shape
    units = rights[0][0].shape[1]
    parts, groups = len(lefts), len(rights)
    rows = width // owners
    step = owners_at_once(rows)
    tile = step * rows

    def kernel(*refs):
        left = refs[:parts]
        right = refs[parts : parts + parts * groups]
        out = refs[-1]
        for g in range(groups):
            total = None
            for p in range(parts):
                part = contract(left[p][...], right[g * parts + p][...], 0, 0)
                total = part if total is None else total + part
            out[:, g] = total.astype(bf16).reshape(step, rows, units)

    left_spec = pl.BlockSpec((tokens, tile), lambda n: (0, n))
    right_spec = pl.BlockSpec((tokens, units), lambda n: (0, 0))
    return pl.pallas_call(
        kernel,
        out_shape=jax.ShapeDtypeStruct((owners, groups, rows, units), bf16),
        grid=(width // tile,),
        in_specs=[left_spec] * parts + [right_spec] * (parts * groups),
        out_specs=pl.BlockSpec((step, groups, rows, units), lambda n: (n, 0, 0, 0)),
        compiler_params=pltpu.CompilerParams(vmem_limit_bytes=40 * 1024 * 1024),
        cost_estimate=pl.CostEstimate(
            flops=2 * parts * groups * tokens * width * units,
            bytes_accessed=2 * (parts * groups * tokens + groups * width) * units,
            transcendentals=0,
        ),
        name="weight_grads",
    )(*lefts, *[value for group in rights for value in group])


def pack_ups(output, query, latent):
    lanes = output.shape[1]
    rest = query[:, lanes:]
    rest = jnp.pad(rest, ((0, 0), (0, lanes - rest.shape[1])))
    return jnp.concatenate(
        [output, query[:, :lanes], rest, latent[:, :lanes], latent[:, lanes:]], axis=0
    )


def unpack_ups(packed, output_shape, query_shape, latent_shape):
    lanes = output_shape[1]
    at = output_shape[0]
    query_rows, latent_rows = query_shape[0], latent_shape[0]
    output = packed[..., :at, :]
    query = jnp.concatenate(
        [
            packed[..., at : at + query_rows, :],
            packed[..., at + query_rows : at + 2 * query_rows, : query_shape[1] - lanes],
        ],
        axis=-1,
    )
    at += 2 * query_rows
    latent = jnp.concatenate(
        [packed[..., at : at + latent_rows, :], packed[..., at + latent_rows :, :]], axis=-1
    )
    return output, query, latent


def ups_grads(grad_attn, attended, query_normed, query_grads, latent, pair_grad, owners):
    parts = len(grad_attn)
    tokens, width = grad_attn[0].shape
    lanes = attended[0].shape[0]
    rows, query_rows, latent_rows = (
        size // owners for size in (width, query_normed.shape[0], latent.shape[0])
    )
    columns = query_grads[0].shape[0]
    step = owners_at_once(rows)
    all_rows = rows + 2 * query_rows + 2 * latent_rows
    keys = latent.shape[1]

    def kernel(*refs):
        grads, refs = refs[:parts], refs[parts:]
        outs, refs = refs[:parts], refs[parts:]
        normed, refs = refs[0], refs[1:]
        queries, refs = refs[:parts], refs[parts:]
        latent, pairs, out = refs
        total, query = None, None
        for i in range(parts):
            part = contract(grads[i][...], outs[i][...], 0, 1)
            total = part if total is None else total + part
            part = contract(normed[:, i * tokens : (i + 1) * tokens], queries[i][...], 1, 1)
            query = part if query is None else query + part
        out[:, :rows, :] = total.astype(bf16).reshape(step, rows, lanes)
        query = query.astype(bf16).reshape(step, query_rows, columns)
        at = rows
        out[:, at : at + query_rows, :] = query[:, :, :lanes]
        at += query_rows
        out[:, at : at + query_rows, : columns - lanes] = query[:, :, lanes:]
        out[:, at : at + query_rows, columns - lanes :] = jnp.zeros(
            (step, query_rows, 2 * lanes - columns), bf16
        )
        at += query_rows
        both = jnp.dot(latent[...], pairs[...], preferred_element_type=f32)
        both = both.astype(bf16).reshape(step, latent_rows, 2 * lanes)
        out[:, at : at + latent_rows, :] = both[:, :, :lanes]
        at += latent_rows
        out[:, at : at + latent_rows, :] = both[:, :, lanes:]

    def fixed(shape):
        return pl.BlockSpec(shape, lambda n: (0, 0))

    return pl.pallas_call(
        kernel,
        out_shape=jax.ShapeDtypeStruct((owners, all_rows, lanes), bf16),
        grid=(owners // step,),
        in_specs=[pl.BlockSpec((tokens, step * rows), lambda n: (0, n))] * parts
        + [fixed((lanes, tokens))] * parts
        + [pl.BlockSpec((step * query_rows, parts * tokens), lambda n: (n, 0))]
        + [fixed((columns, tokens))] * parts
        + [pl.BlockSpec((step * latent_rows, keys), lambda n: (n, 0)), fixed(pair_grad.shape)],
        out_specs=pl.BlockSpec((step, all_rows, lanes), lambda n: (n, 0, 0)),
        compiler_params=pltpu.CompilerParams(vmem_limit_bytes=40 * 1024 * 1024),
        cost_estimate=pl.CostEstimate(
            flops=2 * parts * tokens * (width * lanes + query_normed.shape[0] * columns)
            + 4 * keys * latent.shape[0] * lanes,
            bytes_accessed=2 * (owners * all_rows * lanes + keys * lanes * 2),
            transcendentals=0,
        ),
        name="ups_grads",
    )(*grad_attn, *attended, query_normed, *query_grads, latent, pair_grad)


def held(*values):
    out = lax.optimization_barrier(values)
    return out if len(values) > 1 else out[0]


class Order:
    def __init__(self):
        self.last = None

    def take(self, *values):
        if self.last is not None:
            values = lax.optimization_barrier((*values, self.last))[:-1]
        return values if len(values) > 1 else values[0]

    def mark(self, value):
        self.last = value
        return value


def low_sum_of(left, right):
    return (left.astype(f32) + right.astype(f32)).astype(bf16)


class LinePipe:
    def __init__(self, order):
        self.order = order
        self.direct = lax.axis_size("tensor") != 4
        index = lax.axis_index("tensor")
        self.inner = (index == 1) | (index == 2)
        self.waiting = []
        self.entered = None
        self.crossed = None
        self.left = None
        self.sums = {}
        self.count = 0

    def push(self, part, pieces, ahead=False):
        rows = part.shape[0] // pieces
        keys = []
        fresh = []
        for i in range(pieces):
            piece = part[i * rows : (i + 1) * rows]
            keys.append(self.count)
            if self.direct:
                total = lax.psum(piece, "tensor")
                self.sums[self.count] = (total, total)
            else:
                fresh.append((self.count, piece))
            self.count += 1
        self.waiting = fresh + self.waiting if ahead else self.waiting + fresh
        return keys

    def step(self, *others):
        if self.direct:
            return others if len(others) != 1 else others[0]
        arrived = []
        if self.entered is not None:
            arrived += [self.entered[1], self.entered[2]]
        if self.crossed is not None:
            arrived += [self.crossed[1], self.crossed[2]]
        fresh = self.waiting.pop(0) if self.waiting else None
        if fresh is not None:
            arrived.append(fresh[1])
        if self.left is not None:
            others = others + (self.left,)
        taken = self.order.take(*arrived, *others)
        if len(arrived) + len(others) == 1:
            taken = (taken,)
        taken = list(taken)
        if self.left is not None:
            taken.pop()
        half = whole = None
        if self.entered is not None:
            half = low_sum_of(taken.pop(0), taken.pop(0))
        if self.crossed is not None:
            whole = low_sum_of(taken.pop(0), taken.pop(0))
        low = taken.pop(0) if fresh is not None else None
        joint = whole is not None and low is not None and whole.shape == low.shape
        sends = [value for value in (half, whole) if value is not None]
        if joint:
            sends.append(jnp.where(self.inner, whole, low))
        elif low is not None:
            sends.append(low)
        if sends:
            sends = lax.optimization_barrier(tuple(sends))
            self.order.mark(sends[-1])
        sends = list(sends)
        half = sends.pop(0) if half is not None else None
        whole = sends.pop(0) if whole is not None else None
        crossed, entered, left = None, None, None
        inwards, outwards = [(0, 1), (3, 2)], [(1, 0), (2, 3)]
        if joint:
            got = lax.ppermute(sends[0], "tensor", inwards + outwards)
            self.sums[self.crossed[0]] = (whole, got)
            entered = (fresh[0], sends[0], got)
        else:
            if whole is not None:
                got = left = lax.ppermute(whole, "tensor", outwards)
                self.sums[self.crossed[0]] = (whole, got)
            if low is not None:
                entered = (fresh[0], sends[0], lax.ppermute(sends[0], "tensor", inwards))
        if joint:
            entered = (fresh[0], low, got)
        if half is not None:
            crossed = (self.entered[0], half, lax.ppermute(half, "tensor", [(1, 2), (2, 1)]))
        self.entered, self.crossed, self.left = entered, crossed, left
        return taken if len(taken) != 1 else taken[0]

    def done(self, keys):
        pieces = [jnp.where(self.inner, *self.sums[key]) for key in keys]
        return jnp.concatenate(pieces, axis=0)


def from_others(rows):
    count = lax.axis_size("ctx")
    return [
        lax.ppermute(rows, "ctx", [((i + k) % count, i) for i in range(count)])
        for k in range(1, count)
    ]


def back_to_owners(blocks):
    count = lax.axis_size("ctx")
    total = blocks[0].astype(f32)
    for k in range(1, count):
        total = total + lax.ppermute(
            blocks[k], "ctx", [(i, (i + k) % count) for i in range(count)]
        ).astype(f32)
    return total


def per_device(
    layer_input,
    cotangent,
    span_order,
    query_down,
    latent_down,
    query_up,
    latent_up,
    output_weight,
    gate_weight,
    up_weight,
    down_weight,
    first_gain,
    query_gain,
    latent_gain,
    second_gain,
):
    ctx_count = lax.axis_size("ctx")
    tensor_count = lax.axis_size("tensor")
    ctx_index = lax.axis_index("ctx")
    part_index = lax.axis_index("tensor")
    tokens = layer_input.shape[1]
    spans = span_order.shape[0] // ctx_count
    span = tokens // spans
    width = layer_input.shape[2]
    chunks = [slice(i * span, (i + 1) * span) for i in range(spans)]
    weights_at = ("dp", "ctx")
    order = Order()

    owners = weights_count()
    down_both = lax.all_gather(
        jnp.concatenate([query_down, latent_down], axis=1), weights_at, axis=0, tiled=True
    )
    inputs = layer_input[0]
    normed_one, factor_one = rms_norm(inputs.astype(f32), first_gain, -1)
    norm_one = normed_one.astype(bf16)
    output_rows = output_weight.T
    shapes = [output_rows.shape, query_up.shape, latent_up.shape]
    ups = pack_ups(output_rows, query_up, latent_up)
    ups, norm_one = held(ups, norm_one)
    ups = lax.all_gather(ups, weights_at, axis=0)

    places = lax.dynamic_slice_in_dim(
        jnp.concatenate([span_order, span_order]), ctx_index * spans, spans * ctx_count
    )
    local_places = (
        places[:spans, None] * span + jnp.arange(span, dtype=jnp.int32)[None, :]
    ).reshape(-1)
    cosine, sine = angles(local_places, ROPE)

    lowered = contract(down_both, norm_one, 0, 1)
    ffn_weights = jnp.stack([gate_weight, up_weight, down_weight.T])
    ffn_weights, lowered = held(ffn_weights, lowered)
    ffn_weights = lax.all_gather(ffn_weights, weights_at, axis=0)
    query_latent = lowered[:QRANK]
    latent_raw = lowered[QRANK : QRANK + KVRANK]
    latent_normed, latent_factor = rms_norm(latent_raw, latent_gain)
    rotary_key = rotate(lowered[QRANK + KVRANK :], cosine, sine)
    latent_pack = jnp.concatenate([latent_normed, rotary_key], axis=0).astype(bf16)
    ups, latent_pack = held(ups, latent_pack)
    sequence_pack = jnp.concatenate([latent_pack] + from_others(latent_pack), axis=1)
    output_all, query_up_all, latent_up_all = [
        part.reshape(-1, part.shape[-1]) for part in unpack_ups(ups, *shapes)
    ]
    query_normed, query_factor = rms_norm(query_latent, query_gain)
    query_normed = query_normed.astype(bf16)
    query_raw = contract(query_up_all, query_normed, 0, 0)
    sequence_latent = sequence_pack[:KVRANK]
    pairs = contract(sequence_latent, latent_up_all, 0, 0).astype(bf16)
    rotary = jnp.pad(sequence_pack[KVRANK:].T, ((0, 0), (NOPE, PAIR - HEAD)))

    grad_ffn = (depth_scale * cotangent[0].astype(f32)).astype(bf16)
    pipe = LinePipe(order)
    attended, queries, log_totals = [], [], []
    attn_sums = []
    for i, rows in enumerate(chunks):
        raw = order.take(query_raw[:, rows])
        out, query, log_total = attend(
            i, places, raw, cosine[:, rows], sine[:, rows], pairs, rotary
        )
        order.mark(out)
        attended.append(out)
        queries.append(query)
        log_totals.append(log_total)
        if i > 0:
            pipe.step()
        part = contract(order.take(out), output_all, 0, 1).astype(bf16)
        attn_sums.append(pipe.push(order.mark(held(part)), 2))
        pipe.step()
    pipe.step()
    pipe.step()

    def ffn_start(i, rows):
        total = order.take(pipe.done(attn_sums[i]))
        middle = inputs[rows].astype(f32) + depth_scale * total.astype(f32)
        normed_two, factor = rms_norm(middle, second_gain, -1)
        norm_two = order.mark(held(normed_two.astype(bf16)))
        hidden, grad_gate, grad_up = ffn_front(norm_two, grad_ffn[rows], ffn_weights)
        order.mark(hidden)
        return middle, factor, norm_two, hidden, grad_gate, grad_up

    def ffn_end(parts):
        grad_gate, grad_up = order.take(parts[4], parts[5])
        part = rows_product([grad_gate, grad_up], ffn_weights, [0, 1])
        return pipe.push(order.mark(part), 2)

    def reduced(grad):
        return lax.psum_scatter(grad, weights_at, scatter_dimension=0, tiled=grad.ndim == 2)

    mine = ffn_start(0, chunks[0])
    pipe.step()
    norm_sums = [ffn_end(mine)]
    pipe.step()
    theirs = ffn_start(1, chunks[1])
    pipe.step()
    norm_sums.append(ffn_end(theirs))
    middle, factor_two, norm_two, hidden, grad_gate, grad_up = zip(mine, theirs)
    down_grad = weight_grads(
        [order.take(grad_ffn[rows]) for rows in chunks], [list(hidden)], owners
    )
    order.mark(down_grad)
    down_done = reduced(down_grad)
    pipe.step()
    two_grads = weight_grads(
        [order.take(part) for part in norm_two], [list(grad_gate), list(grad_up)], owners
    )
    order.mark(two_grads)
    two_done = reduced(two_grads)
    pipe.step()
    ffn_sums = []
    for i, rows in enumerate(chunks):
        part = rows_product([order.take(hidden[i])], ffn_weights, [2])
        ffn_sums.append(pipe.push(order.mark(part), 2))
    pipe.step()

    grad_middle, grad_attn, second_parts = [], [], []
    query_grads, pair_grad, rotary_grad = [], None, 0.0
    for i, rows in enumerate(chunks):
        total = order.take(pipe.done(norm_sums[i]))
        middle_part, second_part = rms_back(
            total.astype(f32), middle[i], factor_two[i], second_gain, -1
        )
        second_parts.append(second_part)
        grad_middle.append(cotangent[0, rows].astype(f32) + middle_part)
        grad_attn.append(held((depth_scale * grad_middle[i]).astype(bf16)))
        order.mark(grad_attn[i])
        grad_attended = contract(output_all, grad_attn[i], 0, 1).astype(bf16)
        query_grad, pair_grad, rotary_part = attend_back(
            i,
            places,
            queries[i],
            cosine[:, rows],
            sine[:, rows],
            pairs,
            rotary,
            grad_attended,
            attended[i],
            log_totals[i],
            pair_grad,
        )
        order.mark(query_grad)
        query_grads.append(query_grad)
        rotary_grad = rotary_grad + rotary_part[:, NOPE:HEAD]
        pipe.step()
        if i == 0:
            down_done = pipe.step(down_done)
    second_gain_grad = sum(second_parts)

    pack_grad = jnp.concatenate(
        [contract(latent_up_all, pair_grad, 1, 1), rotary_grad.T], axis=0
    ).astype(bf16)
    pack_local = back_to_owners(
        [pack_grad[:, k * tokens : (k + 1) * tokens] for k in range(ctx_count)]
    )
    query_part = contract(query_up_all, jnp.concatenate(query_grads, axis=1), 1, 0)
    low_part = jnp.concatenate([query_part, pack_local], axis=0).astype(bf16)
    low_part, two_done = order.take(low_part, two_done)
    low_part = order.mark(held(low_part))
    low_sums = lax.psum(low_part, "tensor")
    outs_grad = ups_grads(
        [order.take(part) for part in grad_attn],
        attended,
        query_normed,
        query_grads,
        sequence_latent,
        pair_grad,
        owners,
    )
    outs_done = reduced(order.mark(outs_grad))
    pipe.step()
    pipe.step()
    pipe.step()
    both = order.take(low_sums).astype(f32)
    grad_query_latent, query_gain_grad = rms_back(
        both[:QRANK], query_latent, query_factor, query_gain
    )
    grad_latent_normed, latent_gain_grad = rms_back(
        both[QRANK : QRANK + KVRANK], latent_raw, latent_factor, latent_gain
    )
    lowered_grad = jnp.concatenate(
        [grad_query_latent, grad_latent_normed, unrotate(both[QRANK + KVRANK :], cosine, sine)],
        axis=0,
    ).astype(bf16)
    lowered_grad = order.mark(held(lowered_grad))
    query_cols = QRANK // tensor_count
    latent_cols = (KVRANK + ROPE) // tensor_count
    cut = jnp.concatenate(
        [
            lax.dynamic_slice_in_dim(lowered_grad, part_index * query_cols, query_cols, 0),
            lax.dynamic_slice_in_dim(
                lowered_grad, QRANK + part_index * latent_cols, latent_cols, 0
            ),
        ],
        axis=0,
    )
    down_cut = contract(norm_one, cut, 0, 1)
    grad_norm_one = contract(lowered_grad, down_both, 0, 1)
    input_part, first_gain_grad = rms_back(
        grad_norm_one, inputs.astype(f32), factor_one, first_gain, -1
    )
    input_rows = jnp.concatenate(grad_middle, axis=0) + input_part

    gains = jnp.concatenate(
        [query_gain_grad.reshape(owners, -1), latent_gain_grad.reshape(owners, -1)], axis=1
    )
    gains = jnp.pad(gains, ((0, 0), (0, width // owners - gains.shape[1]))).reshape(-1)
    columns = [first_gain_grad[:, None], second_gain_grad[:, None], gains[:, None]]
    last = jnp.concatenate([down_cut] + columns, axis=1).astype(bf16)
    last, outs_done = order.take(last, outs_done)
    last_done = reduced(order.mark(last)).astype(f32)
    qd_done = last_done[:, :query_cols]
    ld_done = last_done[:, query_cols : query_cols + latent_cols]
    first_done = last_done[:, query_cols + latent_cols]
    second_done = last_done[:, query_cols + latent_cols + 1]
    gains_done = last_done[:, query_cols + latent_cols + 2]
    query_done = gains_done[: QRANK // owners]
    latent_done = gains_done[QRANK // owners : (QRANK + KVRANK) // owners]
    out_done, qu_done, lu_done = unpack_ups(outs_done.astype(f32), *shapes)
    out_done = out_done.T
    two_done = two_done.astype(f32)

    block_rows = [
        (middle[i] + depth_scale * pipe.done(ffn_sums[i]).astype(f32)).astype(bf16)
        for i in range(spans)
    ]
    return (
        jnp.concatenate(block_rows, axis=0)[None],
        input_rows[None],
        qd_done,
        ld_done,
        qu_done,
        lu_done,
        out_done,
        two_done[0],
        two_done[1],
        down_done[0].astype(f32).T,
        first_done,
        query_done,
        latent_done,
        second_done,
    )


def weights_count():
    return lax.axis_size("dp") * lax.axis_size("ctx")


def solution(mesh):
    placed = (
        P("dp", "ctx", None),
        P("dp", "ctx", None),
        P(),
        P(("dp", "ctx"), None),
        P(("dp", "ctx"), None),
        P(("dp", "ctx"), "tensor"),
        P(("dp", "ctx"), "tensor"),
        P("tensor", ("dp", "ctx")),
        P(("dp", "ctx"), "tensor"),
        P(("dp", "ctx"), "tensor"),
        P("tensor", ("dp", "ctx")),
        P(),
        P(),
        P(),
        P(),
    )
    return jax.shard_map(
        per_device,
        mesh=mesh,
        in_specs=placed,
        out_specs=(
            P("dp", "ctx", None),
            P("dp", "ctx", None),
            P(("dp", "ctx"), "tensor"),
            P(("dp", "ctx"), "tensor"),
            P(("dp", "ctx"), "tensor"),
            P(("dp", "ctx"), "tensor"),
            P("tensor", ("dp", "ctx")),
            P(("dp", "ctx"), "tensor"),
            P(("dp", "ctx"), "tensor"),
            P("tensor", ("dp", "ctx")),
            P(("dp", "ctx")),
            P(("dp", "ctx")),
            P(("dp", "ctx")),
            P(("dp", "ctx")),
        ),
        check_vma=False,
    )
```

```python
import math

import jax
import jax.numpy as jnp
from jax import lax
from jax.experimental import pallas as pl
from jax.experimental.pallas import tpu as pltpu
from jax.sharding import PartitionSpec as P

NOPE = 64
ROPE = 32
VDIM = 64
QRANK = 768
KVRANK = 256
HEAD = NOPE + ROPE
PAIR = NOPE + VDIM

depth_scale = 1.4 / math.sqrt(62.0)
eps_value = 1e-05
masked_value = -1e30
score_scale = 1.0 / math.sqrt(NOPE + ROPE)
log2_scale = score_scale / math.log(2.0)

f32 = jnp.float32
bf16 = jnp.bfloat16


def contract(left, right, left_dim, right_dim):
    return lax.dot_general(
        left, right, (((left_dim,), (right_dim,)), ((), ())), preferred_element_type=f32
    )


def rms_norm(values, gain, axis=0):
    factor = lax.rsqrt(jnp.mean(values * values, axis=axis, keepdims=True) + eps_value)
    gain = gain[:, None] if axis == 0 else gain
    return (values * factor * gain, factor)


def rms_back(grad_out, values, factor, gain, axis=0):
    normed = values * factor
    scaled = grad_out * (gain[:, None] if axis == 0 else gain)
    grad_in = factor * (scaled - normed * jnp.mean(scaled * normed, axis=axis, keepdims=True))
    return (grad_in, jnp.sum(grad_out * normed, axis=axis + 1))


def angles(places, width):
    half_width = width // 2
    spectrum = 10000.0 ** (-2.0 * jnp.arange(half_width, dtype=jnp.float32) / width)
    turned = spectrum[:, None] * places.astype(jnp.float32)[None, :]
    return (jnp.cos(turned), jnp.sin(turned))


def rotate(values, cosine, sine):
    half = values.shape[0] // 2
    former, latter = values[:half], values[half:]
    return jnp.concatenate(
        [former * cosine - latter * sine, latter * cosine + former * sine], axis=0
    )


def unrotate(values, cosine, sine):
    half = values.shape[0] // 2
    former, latter = values[:half], values[half:]
    return jnp.concatenate(
        [former * cosine + latter * sine, latter * cosine - former * sine], axis=0
    )


def joined_keys(pairs, rotary):
    lane = lax.broadcasted_iota(jnp.int32, pairs.shape, 1)
    return jnp.where(lane < NOPE, pairs, rotary)


def attend_kernel(blocks, span, own, places, query_raw, cosine, sine, pairs, rotary, out, query_out, log_out, top, total, acc):
    half = ROPE // 2
    former = query_raw[NOPE : NOPE + half, :]
    latter = query_raw[NOPE + half :, :]
    query = jnp.concatenate(
        [
            query_raw[:NOPE, :],
            former * cosine[...] - latter * sine[...],
            latter * cosine[...] + former * sine[...],
        ],
        axis=0,
    ).astype(bf16)
    query_out[...] = query
    top[...] = jnp.full(top.shape, masked_value, f32)
    total[...] = jnp.zeros(total.shape, f32)
    acc[...] = jnp.zeros(acc.shape, f32)
    mine = places[own]

    def visit(block, diagonal):
        rows = pl.ds(block * span, span)
        pair = pairs[rows, :]
        key = joined_keys(pair, rotary[rows, :])[:, :HEAD]
        scores = contract(key, query, 1, 0)
        if diagonal:
            key_at = lax.broadcasted_iota(jnp.int32, scores.shape, 0)
            query_at = lax.broadcasted_iota(jnp.int32, scores.shape, 1)
            scores = jnp.where(key_at <= query_at, scores, masked_value)
        before = top[...]
        highest = jnp.maximum(before, jnp.max(scores, axis=0, keepdims=True))
        expo = jnp.exp2((scores - highest) * log2_scale)
        shrink = jnp.exp2((before - highest) * log2_scale)
        top[...] = highest
        total[...] = total[...] * shrink + jnp.sum(expo, axis=0, keepdims=True)
        acc[...] = acc[...] * shrink + contract(pair, expo.astype(bf16), 0, 0)

    for block in range(blocks):
        theirs = places[block]
        pl.when(theirs < mine)(lambda block=block: visit(block, False))
        pl.when(theirs == mine)(lambda block=block: visit(block, True))
    out[...] = (acc[NOPE:, :] / total[...]).astype(bf16)
    log_out[0] = top[...] * log2_scale + jnp.log2(total[...])


def attend(own, places, query_raw, cosine, sine, pairs, rotary):
    rows, tokens = query_raw.shape
    heads = rows // HEAD
    keys = pairs.shape[0]
    span = tokens
    blocks = keys // span
    elements = heads * tokens * keys
    half = ROPE // 2

    def kernel(*refs):
        attend_kernel(blocks, span, own, *refs)

    return pl.pallas_call(
        kernel,
        out_shape=(
            jax.ShapeDtypeStruct((heads * VDIM, tokens), bf16),
            jax.ShapeDtypeStruct((rows, tokens), bf16),
            jax.ShapeDtypeStruct((heads, 1, tokens), f32),
        ),
        grid_spec=pltpu.PrefetchScalarGridSpec(
            num_scalar_prefetch=1,
            grid=(heads,),
            in_specs=[
                pl.BlockSpec((HEAD, tokens), lambda h, p: (h, 0)),
                pl.BlockSpec((half, tokens), lambda h, p: (0, 0)),
                pl.BlockSpec((half, tokens), lambda h, p: (0, 0)),
                pl.BlockSpec((keys, PAIR), lambda h, p: (0, h)),
                pl.BlockSpec((keys, PAIR), lambda h, p: (0, 0)),
            ],
            out_specs=(
                pl.BlockSpec((VDIM, tokens), lambda h, p: (h, 0)),
                pl.BlockSpec((HEAD, tokens), lambda h, p: (h, 0)),
                pl.BlockSpec((1, 1, tokens), lambda h, p: (h, 0, 0)),
            ),
            scratch_shapes=[
                pltpu.VMEM((1, tokens), f32),
                pltpu.VMEM((1, tokens), f32),
                pltpu.VMEM((PAIR, tokens), f32),
            ],
        ),
        compiler_params=pltpu.CompilerParams(vmem_limit_bytes=32 * 1024 * 1024),
        cost_estimate=pl.CostEstimate(
            flops=4 * elements * 128, bytes_accessed=keys * heads * PAIR * 2, transcendentals=elements
        ),
        name="attend",
    )(places, query_raw, cosine, sine, pairs, rotary)


def attend_back_kernel(blocks, span, start, own, places, query_in, cosine, sine, pairs, rotary, grad_in, out_in, log_in, *rest):
    if start:
        base, query_grad, pair_grad, rotary_grad, acc = rest
    else:
        query_grad, pair_grad, rotary_grad, acc = rest
    half = ROPE // 2
    mine = places[own]
    query = query_in[...]
    grad = grad_in[...]
    inner = jnp.sum(grad.astype(f32) * out_in[...].astype(f32), axis=0, keepdims=True)
    grad_tall = jnp.concatenate([jnp.zeros((NOPE, grad.shape[1]), bf16), grad], axis=0)
    query_tall = jnp.concatenate([query, jnp.zeros((PAIR - HEAD, grad.shape[1]), bf16)], axis=0)
    log_total = log_in[0]
    acc[...] = jnp.zeros(acc.shape, f32)

    @pl.when(pl.program_id(0) == 0)
    def _():
        rotary_grad[...] = jnp.zeros(rotary_grad.shape, f32)

    def visit(block, diagonal):
        rows = pl.ds(block * span, span)
        pair = pairs[rows, :]
        key = joined_keys(pair, rotary[rows, :])
        scores = contract(key, query_tall, 1, 0)
        probs = jnp.exp2(scores * log2_scale - log_total)
        if diagonal:
            key_at = lax.broadcasted_iota(jnp.int32, scores.shape, 0)
            query_at = lax.broadcasted_iota(jnp.int32, scores.shape, 1)
            probs = jnp.where(key_at <= query_at, probs, 0.0)
        grad_probs = contract(pair, grad_tall, 1, 0)
        grad_scores = (probs * (grad_probs - inner)).astype(bf16)
        key_part = contract(grad_scores, query_tall, 1, 1) * score_scale
        value_part = contract(probs.astype(bf16), grad_tall, 1, 1)
        lane = lax.broadcasted_iota(jnp.int32, key_part.shape, 1)
        both = jnp.where(lane < NOPE, key_part, value_part)
        if start:
            both = both + base[rows, :].astype(f32)
        pair_grad[rows, :] = both.astype(bf16)
        rotary_grad[rows, :] += key_part
        acc[...] += contract(key, grad_scores, 0, 0)

    def skip(block):
        rows = pl.ds(block * span, span)
        if start:
            pair_grad[rows, :] = base[rows, :]
        else:
            pair_grad[rows, :] = jnp.zeros((span, PAIR), bf16)

    for block in range(blocks):
        theirs = places[block]
        pl.when(theirs < mine)(lambda block=block: visit(block, False))
        pl.when(theirs == mine)(lambda block=block: visit(block, True))
        pl.when(theirs > mine)(lambda block=block: skip(block))
    total = acc[...] * score_scale
    former = total[NOPE : NOPE + half, :]
    latter = total[NOPE + half : HEAD, :]
    query_grad[...] = jnp.concatenate(
        [
            total[:NOPE, :],
            former * cosine[...] + latter * sine[...],
            latter * cosine[...] - former * sine[...],
        ],
        axis=0,
    ).astype(bf16)


def attend_back(own, places, query, cosine, sine, pairs, rotary, grad, out, log_total, base):
    rows, tokens = query.shape
    heads = rows // HEAD
    keys = pairs.shape[0]
    span = tokens
    blocks = keys // span
    elements = heads * tokens * keys
    half = ROPE // 2
    start = base is not None

    def kernel(*refs):
        attend_back_kernel(blocks, span, start, own, *refs)

    args = [places, query, cosine, sine, pairs, rotary, grad, out, log_total]
    in_specs = [
        pl.BlockSpec((HEAD, tokens), lambda h, p: (h, 0)),
        pl.BlockSpec((half, tokens), lambda h, p: (0, 0)),
        pl.BlockSpec((half, tokens), lambda h, p: (0, 0)),
        pl.BlockSpec((keys, PAIR), lambda h, p: (0, h)),
        pl.BlockSpec((keys, PAIR), lambda h, p: (0, 0)),
        pl.BlockSpec((VDIM, tokens), lambda h, p: (h, 0)),
        pl.BlockSpec((VDIM, tokens), lambda h, p: (h, 0)),
        pl.BlockSpec((1, 1, tokens), lambda h, p: (h, 0, 0)),
    ]
    if start:
        args.append(base)
        in_specs.append(pl.BlockSpec((keys, PAIR), lambda h, p: (0, h)))
    return pl.pallas_call(
        kernel,
        out_shape=(
            jax.ShapeDtypeStruct((rows, tokens), bf16),
            jax.ShapeDtypeStruct((keys, heads * PAIR), bf16),
            jax.ShapeDtypeStruct((keys, PAIR), f32),
        ),
        grid_spec=pltpu.PrefetchScalarGridSpec(
            num_scalar_prefetch=1,
            grid=(heads,),
            in_specs=in_specs,
            out_specs=(
                pl.BlockSpec((HEAD, tokens), lambda h, p: (h, 0)),
                pl.BlockSpec((keys, PAIR), lambda h, p: (0, h)),
                pl.BlockSpec((keys, PAIR), lambda h, p: (0, 0)),
            ),
            scratch_shapes=[pltpu.VMEM((PAIR, tokens), f32)],
        ),
        compiler_params=pltpu.CompilerParams(vmem_limit_bytes=32 * 1024 * 1024),
        cost_estimate=pl.CostEstimate(
            flops=10 * elements * 128, bytes_accessed=keys * heads * PAIR * 4, transcendentals=elements
        ),
        name="attend_back",
    )(*args)


def ffn_front(normed, grad, weights, tile=256):
    tokens, width = normed.shape
    owners, kinds, rows, units = weights.shape

    def kernel(normed, grad, gate, up, down, hidden, grad_gate, grad_up):
        def product(left, weight):
            weight = weight[...].reshape(width, tile)
            return jnp.dot(left[...], weight, preferred_element_type=f32)

        gate_value = product(normed, gate)
        up_value = product(normed, up)
        grad_hidden = product(grad, down)
        sigma = jax.nn.sigmoid(gate_value)
        silu_gate = gate_value * sigma
        hidden[...] = (silu_gate * up_value).astype(bf16)
        slope = sigma * (1.0 + gate_value * (1.0 - sigma))
        grad_gate[...] = (grad_hidden * up_value * slope).astype(bf16)
        grad_up[...] = (grad_hidden * silu_gate).astype(bf16)

    whole = pl.BlockSpec((tokens, width), lambda n: (0, 0))
    weight = [
        pl.BlockSpec((owners, None, rows, tile), lambda n, kind=kind: (0, kind, 0, n))
        for kind in range(kinds)
    ]
    given = jax.ShapeDtypeStruct((tokens, units), bf16)
    block = pl.BlockSpec((tokens, tile), lambda n: (0, n))
    return pl.pallas_call(
        kernel,
        out_shape=(given, given, given),
        grid=(pl.cdiv(units, tile),),
        in_specs=[whole, whole] + weight,
        out_specs=(block, block, block),
        compiler_params=pltpu.CompilerParams(vmem_limit_bytes=40 * 1024 * 1024),
        cost_estimate=pl.CostEstimate(
            flops=6 * tokens * width * units,
            bytes_accessed=6 * width * units,
            transcendentals=tokens * units,
        ),
        name="ffn_front",
    )(normed, grad, weights, weights, weights)


def owners_at_once(rows):
    step = 1
    while step * rows % 128:
        step += 1
    return step


def rows_product(lefts, weights, kinds):
    tokens, units = lefts[0].shape
    owners, _, rows, _ = weights.shape
    step = owners_at_once(rows)
    tile = step * rows
    width = owners * rows
    count = len(lefts)

    def kernel(*refs):
        total = None
        for i in range(count):
            weight = refs[count + i][...].reshape(tile, units)
            part = contract(refs[i][...], weight, 1, 1)
            total = part if total is None else total + part
        refs[-1][...] = total.astype(bf16)

    whole = pl.BlockSpec((tokens, units), lambda n: (0, 0))
    weight = [
        pl.BlockSpec((step, None, rows, units), lambda n, kind=kind: (n, kind, 0, 0))
        for kind in kinds
    ]
    return pl.pallas_call(
        kernel,
        out_shape=jax.ShapeDtypeStruct((tokens, width), bf16),
        grid=(width // tile,),
        in_specs=[whole] * count + weight,
        out_specs=pl.BlockSpec((tokens, tile), lambda n: (0, n)),
        compiler_params=pltpu.CompilerParams(vmem_limit_bytes=40 * 1024 * 1024),
        cost_estimate=pl.CostEstimate(
            flops=2 * count * tokens * width * units,
            bytes_accessed=2 * count * width * units,
            transcendentals=0,
        ),
        name="rows_product",
    )(*lefts, *([weights] * count))


def weight_grads(groups, owners):
    lefts = []
    for left, _ in groups:
        if not any(left is other for other in lefts):
            lefts.append(left)
    which = [[left is other for other in lefts].index(True) for left, _ in groups]
    parts = len(lefts[0])
    tokens, width = lefts[0][0].shape
    units = groups[0][1][0].shape[1]
    count = len(groups)
    rows = width // owners
    step = owners_at_once(rows)
    tile = step * rows

    def kernel(*refs):
        left = refs[: parts * len(lefts)]
        right = refs[parts * len(lefts) : -1]
        out = refs[-1]
        for g in range(count):
            total = None
            for p in range(parts):
                part = contract(
                    left[which[g] * parts + p][...], right[g * parts + p][...], 0, 0
                )
                total = part if total is None else total + part
            out[:, g] = total.astype(bf16).reshape(step, rows, units)

    left_spec = pl.BlockSpec((tokens, tile), lambda n: (0, n))
    right_spec = pl.BlockSpec(
        (tokens, units), lambda n: (0, 0), pipeline_mode=pl.Buffered(buffer_count=1)
    )
    return pl.pallas_call(
        kernel,
        out_shape=jax.ShapeDtypeStruct((owners, count, rows, units), bf16),
        grid=(width // tile,),
        in_specs=[left_spec] * (parts * len(lefts)) + [right_spec] * (parts * count),
        out_specs=pl.BlockSpec((step, count, rows, units), lambda n: (n, 0, 0, 0)),
        compiler_params=pltpu.CompilerParams(vmem_limit_bytes=44 * 1024 * 1024),
        cost_estimate=pl.CostEstimate(
            flops=2 * parts * count * tokens * width * units,
            bytes_accessed=2 * (parts * count * tokens + count * width) * units,
            transcendentals=0,
        ),
        name="weight_grads",
    )(*[part for left in lefts for part in left], *[part for _, right in groups for part in right])


def pack_ups(output, query, latent):
    lanes = output.shape[1]
    rest = query[:, lanes:]
    rest = jnp.pad(rest, ((0, 0), (0, lanes - rest.shape[1])))
    return jnp.concatenate(
        [output, query[:, :lanes], rest, latent[:, :lanes], latent[:, lanes:]], axis=0
    )


def unpack_ups(packed, output_shape, query_shape, latent_shape):
    lanes = output_shape[1]
    at = output_shape[0]
    query_rows, latent_rows = query_shape[0], latent_shape[0]
    output = packed[..., :at, :]
    query = jnp.concatenate(
        [
            packed[..., at : at + query_rows, :],
            packed[..., at + query_rows : at + 2 * query_rows, : query_shape[1] - lanes],
        ],
        axis=-1,
    )
    at += 2 * query_rows
    latent = jnp.concatenate(
        [packed[..., at : at + latent_rows, :], packed[..., at + latent_rows :, :]], axis=-1
    )
    return output, query, latent


def ups_grads(grad_attn, attended, query_normed, query_grads, latent, pair_grad, owners):
    parts = len(grad_attn)
    tokens, width = grad_attn[0].shape
    lanes = attended[0].shape[0]
    rows, query_rows, latent_rows = (
        size // owners for size in (width, query_normed.shape[0], latent.shape[0])
    )
    columns = query_grads[0].shape[0]
    step = owners_at_once(rows)
    all_rows = rows + 2 * query_rows + 2 * latent_rows
    keys = latent.shape[1]

    def kernel(*refs):
        grads, refs = refs[:parts], refs[parts:]
        outs, refs = refs[:parts], refs[parts:]
        normed, refs = refs[0], refs[1:]
        queries, refs = refs[:parts], refs[parts:]
        latent, pairs, out = refs
        total, query = None, None
        for i in range(parts):
            part = contract(grads[i][...], outs[i][...], 0, 1)
            total = part if total is None else total + part
            part = contract(normed[:, i * tokens : (i + 1) * tokens], queries[i][...], 1, 1)
            query = part if query is None else query + part
        out[:, :rows, :] = total.astype(bf16).reshape(step, rows, lanes)
        query = query.astype(bf16).reshape(step, query_rows, columns)
        at = rows
        out[:, at : at + query_rows, :] = query[:, :, :lanes]
        at += query_rows
        out[:, at : at + query_rows, : columns - lanes] = query[:, :, lanes:]
        out[:, at : at + query_rows, columns - lanes :] = jnp.zeros(
            (step, query_rows, 2 * lanes - columns), bf16
        )
        at += query_rows
        both = jnp.dot(latent[...], pairs[...], preferred_element_type=f32)
        both = both.astype(bf16).reshape(step, latent_rows, 2 * lanes)
        out[:, at : at + latent_rows, :] = both[:, :, :lanes]
        at += latent_rows
        out[:, at : at + latent_rows, :] = both[:, :, lanes:]

    def fixed(shape):
        return pl.BlockSpec(shape, lambda n: (0, 0))

    return pl.pallas_call(
        kernel,
        out_shape=jax.ShapeDtypeStruct((owners, all_rows, lanes), bf16),
        grid=(owners // step,),
        in_specs=[pl.BlockSpec((tokens, step * rows), lambda n: (0, n))] * parts
        + [fixed((lanes, tokens))] * parts
        + [pl.BlockSpec((step * query_rows, parts * tokens), lambda n: (n, 0))]
        + [fixed((columns, tokens))] * parts
        + [pl.BlockSpec((step * latent_rows, keys), lambda n: (n, 0)), fixed(pair_grad.shape)],
        out_specs=pl.BlockSpec((step, all_rows, lanes), lambda n: (n, 0, 0)),
        compiler_params=pltpu.CompilerParams(vmem_limit_bytes=40 * 1024 * 1024),
        cost_estimate=pl.CostEstimate(
            flops=2 * parts * tokens * (width * lanes + query_normed.shape[0] * columns)
            + 4 * keys * latent.shape[0] * lanes,
            bytes_accessed=2 * (owners * all_rows * lanes + keys * lanes * 2),
            transcendentals=0,
        ),
        name="ups_grads",
    )(*grad_attn, *attended, query_normed, *query_grads, latent, pair_grad)


def held(*values):
    out = lax.optimization_barrier(values)
    return out if len(values) > 1 else out[0]


class Order:
    def __init__(self):
        self.last = None

    def take(self, *values):
        if self.last is not None:
            values = lax.optimization_barrier((*values, self.last))[:-1]
        return values if len(values) > 1 else values[0]

    def mark(self, value):
        self.last = value
        return value


def low_sum_of(left, right):
    return (left.astype(f32) + right.astype(f32)).astype(bf16)


class LinePipe:
    def __init__(self, order):
        self.order = order
        self.direct = lax.axis_size("tensor") != 4
        index = lax.axis_index("tensor")
        self.inner = (index == 1) | (index == 2)
        self.waiting = []
        self.entered = None
        self.crossed = None
        self.left = None
        self.sums = {}
        self.count = 0

    def push(self, part, pieces, ahead=False):
        rows = part.shape[0] // pieces
        keys = []
        fresh = []
        for i in range(pieces):
            piece = part[i * rows : (i + 1) * rows]
            keys.append(self.count)
            if self.direct:
                total = lax.psum(piece, "tensor")
                self.sums[self.count] = (total, total)
            else:
                fresh.append((self.count, piece))
            self.count += 1
        self.waiting = fresh + self.waiting if ahead else self.waiting + fresh
        return keys

    def step(self, *others):
        if self.direct:
            return others if len(others) != 1 else others[0]
        arrived = []
        if self.entered is not None:
            arrived += [self.entered[1], self.entered[2]]
        if self.crossed is not None:
            arrived += [self.crossed[1], self.crossed[2]]
        fresh = self.waiting.pop(0) if self.waiting else None
        if fresh is not None:
            arrived.append(fresh[1])
        if self.left is not None:
            others = others + (self.left,)
        if not arrived and not others:
            return None
        taken = self.order.take(*arrived, *others)
        if len(arrived) + len(others) == 1:
            taken = (taken,)
        taken = list(taken)
        if self.left is not None:
            taken.pop()
        half = whole = None
        if self.entered is not None:
            half = low_sum_of(taken.pop(0), taken.pop(0))
        if self.crossed is not None:
            whole = low_sum_of(taken.pop(0), taken.pop(0))
        low = taken.pop(0) if fresh is not None else None
        joint = whole is not None and low is not None and whole.shape == low.shape
        sends = [value for value in (half, whole) if value is not None]
        if joint:
            sends.append(jnp.where(self.inner, whole, low))
        elif low is not None:
            sends.append(low)
        if sends:
            sends = lax.optimization_barrier(tuple(sends))
            self.order.mark(sends[-1])
        sends = list(sends)
        half = sends.pop(0) if half is not None else None
        whole = sends.pop(0) if whole is not None else None
        crossed, entered, left = None, None, None
        inwards, outwards = [(0, 1), (3, 2)], [(1, 0), (2, 3)]
        if joint:
            got = lax.ppermute(sends[0], "tensor", inwards + outwards)
            self.sums[self.crossed[0]] = (whole, got)
            entered = (fresh[0], sends[0], got)
        else:
            if whole is not None:
                got = left = lax.ppermute(whole, "tensor", outwards)
                self.sums[self.crossed[0]] = (whole, got)
            if low is not None:
                entered = (fresh[0], sends[0], lax.ppermute(sends[0], "tensor", inwards))
        if joint:
            entered = (fresh[0], low, got)
        if half is not None:
            crossed = (self.entered[0], half, lax.ppermute(half, "tensor", [(1, 2), (2, 1)]))
        self.entered, self.crossed, self.left = entered, crossed, left
        return taken if len(taken) != 1 else taken[0]

    def done(self, keys):
        pieces = [jnp.where(self.inner, *self.sums[key]) for key in keys]
        return jnp.concatenate(pieces, axis=0)


def direct_sum(order, part):
    count = lax.axis_size("tensor")
    if count != 4:
        total = lax.psum(part, "tensor")
        return lambda: total
    index = lax.axis_index("tensor")
    rows = part.shape[0] // count

    def share(k):
        return lax.dynamic_slice_in_dim(part, (index + k) % count * rows, rows, 0)

    shares = held(*[share(k) for k in range(count)])
    order.mark(shares[1])
    got = [
        lax.ppermute(shares[k], "tensor", [(i, (i + k) % count) for i in range(count)])
        for k in (2, 1, 3)
    ]

    def finish():
        mine = order.take(shares[0], *got)
        mine = sum(value.astype(f32) for value in mine).astype(bf16)
        mine = order.mark(held(mine))
        pieces = [mine] + [
            lax.ppermute(mine, "tensor", [((i + k) % count, i) for i in range(count)])
            for k in range(1, count)
        ]
        twice = jnp.concatenate(pieces + pieces, axis=0)
        start = (count - index) % count * rows
        return lax.dynamic_slice_in_dim(twice, start, count * rows, 0)

    return finish


def from_others(rows):
    count = lax.axis_size("ctx")
    return [
        lax.ppermute(rows, "ctx", [((i + k) % count, i) for i in range(count)])
        for k in range(1, count)
    ]


def back_to_owners(blocks):
    count = lax.axis_size("ctx")
    total = blocks[0].astype(f32)
    for k in range(1, count):
        total = total + lax.ppermute(
            blocks[k], "ctx", [(i, (i + k) % count) for i in range(count)]
        ).astype(f32)
    return total


def per_device(
    layer_input,
    cotangent,
    span_order,
    query_down,
    latent_down,
    query_up,
    latent_up,
    output_weight,
    gate_weight,
    up_weight,
    down_weight,
    first_gain,
    query_gain,
    latent_gain,
    second_gain,
):
    ctx_count = lax.axis_size("ctx")
    tensor_count = lax.axis_size("tensor")
    ctx_index = lax.axis_index("ctx")
    part_index = lax.axis_index("tensor")
    tokens = layer_input.shape[1]
    spans = span_order.shape[0] // ctx_count
    span = tokens // spans
    width = layer_input.shape[2]
    chunks = [slice(i * span, (i + 1) * span) for i in range(spans)]
    weights_at = ("dp", "ctx")
    order = Order()

    owners = weights_count()
    down_both = lax.all_gather(
        jnp.concatenate([query_down, latent_down], axis=1), weights_at, axis=0, tiled=True
    )
    inputs = layer_input[0]
    normed_one, factor_one = rms_norm(inputs.astype(f32), first_gain, -1)
    norm_one = normed_one.astype(bf16)
    output_rows = output_weight.T
    shapes = [output_rows.shape, query_up.shape, latent_up.shape]
    ups = pack_ups(output_rows, query_up, latent_up)
    ups, norm_one = held(ups, norm_one)
    ups = lax.all_gather(ups, weights_at, axis=0)

    places = lax.dynamic_slice_in_dim(
        jnp.concatenate([span_order, span_order]), ctx_index * spans, spans * ctx_count
    )
    local_places = (
        places[:spans, None] * span + jnp.arange(span, dtype=jnp.int32)[None, :]
    ).reshape(-1)
    cosine, sine = angles(local_places, ROPE)

    lowered = contract(down_both, norm_one, 0, 1)
    ffn_weights = jnp.stack([gate_weight, up_weight, down_weight.T])
    ffn_weights, lowered = held(ffn_weights, lowered)
    ffn_weights = lax.all_gather(ffn_weights, weights_at, axis=0)
    query_latent = lowered[:QRANK]
    latent_raw = lowered[QRANK : QRANK + KVRANK]
    latent_normed, latent_factor = rms_norm(latent_raw, latent_gain)
    rotary_key = rotate(lowered[QRANK + KVRANK :], cosine, sine)
    latent_pack = jnp.concatenate([latent_normed, rotary_key], axis=0).astype(bf16)
    ups, _ = held(ups, latent_pack)
    sequence_pack = jnp.concatenate([latent_pack] + from_others(latent_pack), axis=1)
    output_all, query_up_all, latent_up_all = [
        part.reshape(-1, part.shape[-1]) for part in unpack_ups(ups, *shapes)
    ]
    query_normed, query_factor = rms_norm(query_latent, query_gain)
    query_normed = query_normed.astype(bf16)
    query_raw = contract(query_up_all, query_normed, 0, 0)
    sequence_latent = sequence_pack[:KVRANK]
    pairs = contract(sequence_latent, latent_up_all, 0, 0).astype(bf16)
    rotary = jnp.pad(sequence_pack[KVRANK:].T, ((0, 0), (NOPE, PAIR - HEAD)))

    grad_ffn = (depth_scale * cotangent[0].astype(f32)).astype(bf16)
    pipe = LinePipe(order)
    attended, queries, log_totals = [], [], []
    attn_sums = []
    for i, rows in enumerate(chunks):
        raw = order.take(query_raw[:, rows])
        out, query, log_total = attend(
            i, places, raw, cosine[:, rows], sine[:, rows], pairs, rotary
        )
        order.mark(out)
        attended.append(out)
        queries.append(query)
        log_totals.append(log_total)
        if i > 0:
            pipe.step()
        part = contract(order.take(out), output_all, 0, 1).astype(bf16)
        attn_sums.append(pipe.push(order.mark(held(part)), 2))
        pipe.step()
    pipe.step()

    def ffn_start(i, rows):
        total = order.take(pipe.done(attn_sums[i]))
        middle = inputs[rows].astype(f32) + depth_scale * total.astype(f32)
        normed_two, factor = rms_norm(middle, second_gain, -1)
        norm_two = order.mark(held(normed_two.astype(bf16)))
        hidden, grad_gate, grad_up = ffn_front(norm_two, grad_ffn[rows], ffn_weights)
        order.mark(hidden)
        return middle, factor, norm_two, hidden, grad_gate, grad_up

    def ffn_end(parts):
        grad_gate, grad_up = order.take(parts[4], parts[5])
        part = rows_product([grad_gate, grad_up], ffn_weights, [0, 1])
        return pipe.push(order.mark(part), 2)

    def reduced(grad):
        return lax.psum_scatter(grad, weights_at, scatter_dimension=0, tiled=grad.ndim == 2)

    def ffn_out(i):
        part = rows_product([order.take(hidden[i])], ffn_weights, [2])
        return order.mark(part)

    mine = ffn_start(0, chunks[0])
    hidden = [mine[3]]
    pipe.step()
    norm_sums = [ffn_end(mine)]
    pipe.step()
    ffn_parts = [ffn_out(0)]
    pipe.step()
    theirs = ffn_start(1, chunks[1])
    pipe.step()
    norm_sums.append(ffn_end(theirs))
    pipe.step()
    middle, factor_two, norm_two, hidden, grad_gate, grad_up = zip(mine, theirs)
    ffn_cots = [order.take(grad_ffn[rows]) for rows in chunks]
    ffn_grads = weight_grads(
        [(norm_two, grad_gate), (norm_two, grad_up), (ffn_cots, hidden)], owners
    )
    order.mark(ffn_grads)
    pipe.step()
    ffn_done = reduced(order.take(ffn_grads))
    ffn_sums = [pipe.push(ffn_parts[0], 2)]

    grad_middle, grad_attn, second_parts = [], [], []
    query_grads, pair_grad, rotary_grad = [], None, 0.0
    for i, rows in enumerate(chunks):
        total = order.take(pipe.done(norm_sums[i]))
        middle_part, second_part = rms_back(
            total.astype(f32), middle[i], factor_two[i], second_gain, -1
        )
        second_parts.append(second_part)
        grad_middle.append(cotangent[0, rows].astype(f32) + middle_part)
        grad_attn.append(held((depth_scale * grad_middle[i]).astype(bf16)))
        order.mark(grad_attn[i])
        grad_attended = contract(output_all, grad_attn[i], 0, 1).astype(bf16)
        query_grad, pair_grad, rotary_part = attend_back(
            i,
            places,
            queries[i],
            cosine[:, rows],
            sine[:, rows],
            pairs,
            rotary,
            grad_attended,
            attended[i],
            log_totals[i],
            pair_grad,
        )
        order.mark(query_grad)
        query_grads.append(query_grad)
        rotary_grad = rotary_grad + rotary_part[:, NOPE:HEAD]
        if i == 0:
            pipe.step()
            ffn_parts.append(ffn_out(1))
            ffn_sums.append(pipe.push(ffn_parts[1], 2))
            pipe.step()
            pipe.step()
    second_gain_grad = sum(second_parts)

    pack_grad = jnp.concatenate(
        [contract(latent_up_all, pair_grad, 1, 1), rotary_grad.T], axis=0
    ).astype(bf16)
    pack_local = back_to_owners(
        [pack_grad[:, k * tokens : (k + 1) * tokens] for k in range(ctx_count)]
    )
    query_part = contract(query_up_all, jnp.concatenate(query_grads, axis=1), 1, 0)
    low_part = jnp.concatenate([query_part, pack_local], axis=0).astype(bf16)
    low_part = order.mark(held(order.take(low_part)))
    low_finish = direct_sum(order, low_part)
    outs_grad = ups_grads(
        [order.take(part) for part in grad_attn],
        attended,
        query_normed,
        query_grads,
        sequence_latent,
        pair_grad,
        owners,
    )
    order.mark(outs_grad)
    low_sums = low_finish()
    outs_grad, ffn_done = order.take(outs_grad, ffn_done)
    outs_done = reduced(outs_grad)
    pipe.step()
    both = order.take(low_sums).astype(f32)
    grad_query_latent, query_gain_grad = rms_back(
        both[:QRANK], query_latent, query_factor, query_gain
    )
    grad_latent_normed, latent_gain_grad = rms_back(
        both[QRANK : QRANK + KVRANK], latent_raw, latent_factor, latent_gain
    )
    lowered_grad = jnp.concatenate(
        [grad_query_latent, grad_latent_normed, unrotate(both[QRANK + KVRANK :], cosine, sine)],
        axis=0,
    ).astype(bf16)
    lowered_grad = order.mark(held(lowered_grad))
    outs_done = pipe.step(outs_done)
    query_cols = QRANK // tensor_count
    latent_cols = (KVRANK + ROPE) // tensor_count
    cut = jnp.concatenate(
        [
            lax.dynamic_slice_in_dim(lowered_grad, part_index * query_cols, query_cols, 0),
            lax.dynamic_slice_in_dim(
                lowered_grad, QRANK + part_index * latent_cols, latent_cols, 0
            ),
        ],
        axis=0,
    )
    down_cut = contract(norm_one, cut, 0, 1)
    grad_norm_one = contract(lowered_grad, down_both, 0, 1)
    _, first_gain_grad = rms_back(
        grad_norm_one, inputs.astype(f32), factor_one, first_gain, -1
    )
    gains = jnp.concatenate(
        [query_gain_grad.reshape(owners, -1), latent_gain_grad.reshape(owners, -1)], axis=1
    )
    gains = jnp.pad(gains, ((0, 0), (0, width // owners - gains.shape[1]))).reshape(-1)
    columns = [first_gain_grad[:, None], second_gain_grad[:, None], gains[:, None]]
    last = jnp.concatenate([down_cut] + columns, axis=1).astype(bf16)
    last = order.take(last)
    last_done = reduced(order.mark(last)).astype(f32)
    grad_norm_one = order.take(grad_norm_one)
    input_part, _ = rms_back(grad_norm_one, inputs.astype(f32), factor_one, first_gain, -1)
    input_rows = jnp.concatenate(grad_middle, axis=0) + input_part
    pipe.step()
    pipe.step()
    qd_done = last_done[:, :query_cols]
    ld_done = last_done[:, query_cols : query_cols + latent_cols]
    first_done = last_done[:, query_cols + latent_cols]
    second_done = last_done[:, query_cols + latent_cols + 1]
    gains_done = last_done[:, query_cols + latent_cols + 2]
    query_done = gains_done[: QRANK // owners]
    latent_done = gains_done[QRANK // owners : (QRANK + KVRANK) // owners]
    out_done, qu_done, lu_done = unpack_ups(outs_done.astype(f32), *shapes)
    out_done = out_done.T
    ffn_done = ffn_done.astype(f32)

    block_rows = [
        (middle[i] + depth_scale * pipe.done(ffn_sums[i]).astype(f32)).astype(bf16)
        for i in range(spans)
    ]
    return (
        jnp.concatenate(block_rows, axis=0)[None],
        input_rows[None],
        qd_done,
        ld_done,
        qu_done,
        lu_done,
        out_done,
        ffn_done[0],
        ffn_done[1],
        ffn_done[2].T,
        first_done,
        query_done,
        latent_done,
        second_done,
    )


def weights_count():
    return lax.axis_size("dp") * lax.axis_size("ctx")


def solution(mesh):
    placed = (
        P("dp", "ctx", None),
        P("dp", "ctx", None),
        P(),
        P(("dp", "ctx"), None),
        P(("dp", "ctx"), None),
        P(("dp", "ctx"), "tensor"),
        P(("dp", "ctx"), "tensor"),
        P("tensor", ("dp", "ctx")),
        P(("dp", "ctx"), "tensor"),
        P(("dp", "ctx"), "tensor"),
        P("tensor", ("dp", "ctx")),
        P(),
        P(),
        P(),
        P(),
    )
    return jax.shard_map(
        per_device,
        mesh=mesh,
        in_specs=placed,
        out_specs=(
            P("dp", "ctx", None),
            P("dp", "ctx", None),
            P(("dp", "ctx"), "tensor"),
            P(("dp", "ctx"), "tensor"),
            P(("dp", "ctx"), "tensor"),
            P(("dp", "ctx"), "tensor"),
            P("tensor", ("dp", "ctx")),
            P(("dp", "ctx"), "tensor"),
            P(("dp", "ctx"), "tensor"),
            P("tensor", ("dp", "ctx")),
            P(("dp", "ctx")),
            P(("dp", "ctx")),
            P(("dp", "ctx")),
            P(("dp", "ctx")),
        ),
        check_vma=False,
    )
```

```python
import math

import jax
import jax.numpy as jnp
from jax import lax
from jax.experimental import pallas as pl
from jax.experimental.pallas import tpu as pltpu
from jax.sharding import PartitionSpec as P

NOPE = 64
ROPE = 32
VDIM = 64
QRANK = 768
KVRANK = 256
HEAD = NOPE + ROPE
PAIR = NOPE + VDIM

depth_scale = 1.4 / math.sqrt(62.0)
eps_value = 1e-05
masked_value = -1e30
score_scale = 1.0 / math.sqrt(NOPE + ROPE)
log2_scale = score_scale / math.log(2.0)

f32 = jnp.float32
bf16 = jnp.bfloat16


def contract(left, right, left_dim, right_dim):
    return lax.dot_general(
        left, right, (((left_dim,), (right_dim,)), ((), ())), preferred_element_type=f32
    )


def rms_norm(values, gain, axis=0):
    factor = lax.rsqrt(jnp.mean(values * values, axis=axis, keepdims=True) + eps_value)
    gain = gain[:, None] if axis == 0 else gain
    return (values * factor * gain, factor)


def rms_back(grad_out, values, factor, gain, axis=0):
    normed = values * factor
    scaled = grad_out * (gain[:, None] if axis == 0 else gain)
    grad_in = factor * (scaled - normed * jnp.mean(scaled * normed, axis=axis, keepdims=True))
    return (grad_in, jnp.sum(grad_out * normed, axis=axis + 1))


def angles(places, width):
    half_width = width // 2
    spectrum = 10000.0 ** (-2.0 * jnp.arange(half_width, dtype=jnp.float32) / width)
    turned = spectrum[:, None] * places.astype(jnp.float32)[None, :]
    return (jnp.cos(turned), jnp.sin(turned))


def rotate(values, cosine, sine):
    half = values.shape[0] // 2
    former, latter = values[:half], values[half:]
    return jnp.concatenate(
        [former * cosine - latter * sine, latter * cosine + former * sine], axis=0
    )


def unrotate(values, cosine, sine):
    half = values.shape[0] // 2
    former, latter = values[:half], values[half:]
    return jnp.concatenate(
        [former * cosine + latter * sine, latter * cosine - former * sine], axis=0
    )


def joined_keys(pairs, rotary):
    lane = lax.broadcasted_iota(jnp.int32, pairs.shape, 1)
    return jnp.where(lane < NOPE, pairs, rotary)


def attend_kernel(blocks, span, own, places, query_raw, cosine, sine, pairs, rotary, out, query_out, log_out, top, total, acc):
    half = ROPE // 2
    former = query_raw[NOPE : NOPE + half, :]
    latter = query_raw[NOPE + half :, :]
    query = jnp.concatenate(
        [
            query_raw[:NOPE, :],
            former * cosine[...] - latter * sine[...],
            latter * cosine[...] + former * sine[...],
        ],
        axis=0,
    ).astype(bf16)
    query_out[...] = query
    top[...] = jnp.full(top.shape, masked_value, f32)
    total[...] = jnp.zeros(total.shape, f32)
    acc[...] = jnp.zeros(acc.shape, f32)
    mine = places[own]

    def visit(block, diagonal):
        rows = pl.ds(block * span, span)
        pair = pairs[rows, :]
        key = joined_keys(pair, rotary[rows, :])[:, :HEAD]
        scores = contract(key, query, 1, 0)
        if diagonal:
            key_at = lax.broadcasted_iota(jnp.int32, scores.shape, 0)
            query_at = lax.broadcasted_iota(jnp.int32, scores.shape, 1)
            scores = jnp.where(key_at <= query_at, scores, masked_value)
        before = top[...]
        highest = jnp.maximum(before, jnp.max(scores, axis=0, keepdims=True))
        expo = jnp.exp2((scores - highest) * log2_scale)
        shrink = jnp.exp2((before - highest) * log2_scale)
        top[...] = highest
        total[...] = total[...] * shrink + jnp.sum(expo, axis=0, keepdims=True)
        acc[...] = acc[...] * shrink + contract(pair, expo.astype(bf16), 0, 0)

    for block in range(blocks):
        theirs = places[block]
        pl.when(theirs < mine)(lambda block=block: visit(block, False))
        pl.when(theirs == mine)(lambda block=block: visit(block, True))
    out[...] = (acc[NOPE:, :] / total[...]).astype(bf16)
    log_out[0] = top[...] * log2_scale + jnp.log2(total[...])


def attend(own, places, query_raw, cosine, sine, pairs, rotary):
    rows, tokens = query_raw.shape
    heads = rows // HEAD
    keys = pairs.shape[0]
    span = tokens
    blocks = keys // span
    elements = heads * tokens * keys
    half = ROPE // 2

    def kernel(*refs):
        attend_kernel(blocks, span, own, *refs)

    return pl.pallas_call(
        kernel,
        out_shape=(
            jax.ShapeDtypeStruct((heads * VDIM, tokens), bf16),
            jax.ShapeDtypeStruct((rows, tokens), bf16),
            jax.ShapeDtypeStruct((heads, 1, tokens), f32),
        ),
        grid_spec=pltpu.PrefetchScalarGridSpec(
            num_scalar_prefetch=1,
            grid=(heads,),
            in_specs=[
                pl.BlockSpec((HEAD, tokens), lambda h, p: (h, 0)),
                pl.BlockSpec((half, tokens), lambda h, p: (0, 0)),
                pl.BlockSpec((half, tokens), lambda h, p: (0, 0)),
                pl.BlockSpec((keys, PAIR), lambda h, p: (0, h)),
                pl.BlockSpec((keys, PAIR), lambda h, p: (0, 0)),
            ],
            out_specs=(
                pl.BlockSpec((VDIM, tokens), lambda h, p: (h, 0)),
                pl.BlockSpec((HEAD, tokens), lambda h, p: (h, 0)),
                pl.BlockSpec((1, 1, tokens), lambda h, p: (h, 0, 0)),
            ),
            scratch_shapes=[
                pltpu.VMEM((1, tokens), f32),
                pltpu.VMEM((1, tokens), f32),
                pltpu.VMEM((PAIR, tokens), f32),
            ],
        ),
        compiler_params=pltpu.CompilerParams(vmem_limit_bytes=32 * 1024 * 1024),
        cost_estimate=pl.CostEstimate(
            flops=4 * elements * 128, bytes_accessed=keys * heads * PAIR * 2, transcendentals=elements
        ),
        name="attend",
    )(places, query_raw, cosine, sine, pairs, rotary)


def attend_back_kernel(blocks, span, start, own, places, query_in, cosine, sine, pairs, rotary, grad_in, out_in, log_in, *rest):
    if start:
        base, query_grad, pair_grad, rotary_grad, acc = rest
    else:
        query_grad, pair_grad, rotary_grad, acc = rest
    half = ROPE // 2
    mine = places[own]
    query = query_in[...]
    grad = grad_in[...]
    inner = jnp.sum(grad.astype(f32) * out_in[...].astype(f32), axis=0, keepdims=True)
    grad_tall = jnp.concatenate([jnp.zeros((NOPE, grad.shape[1]), bf16), grad], axis=0)
    query_tall = jnp.concatenate([query, jnp.zeros((PAIR - HEAD, grad.shape[1]), bf16)], axis=0)
    log_total = log_in[0]
    acc[...] = jnp.zeros(acc.shape, f32)

    @pl.when(pl.program_id(0) == 0)
    def _():
        rotary_grad[...] = jnp.zeros(rotary_grad.shape, f32)

    def visit(block, diagonal):
        rows = pl.ds(block * span, span)
        pair = pairs[rows, :]
        key = joined_keys(pair, rotary[rows, :])
        scores = contract(key, query_tall, 1, 0)
        probs = jnp.exp2(scores * log2_scale - log_total)
        if diagonal:
            key_at = lax.broadcasted_iota(jnp.int32, scores.shape, 0)
            query_at = lax.broadcasted_iota(jnp.int32, scores.shape, 1)
            probs = jnp.where(key_at <= query_at, probs, 0.0)
        grad_probs = contract(pair, grad_tall, 1, 0)
        grad_scores = (probs * (grad_probs - inner)).astype(bf16)
        key_part = contract(grad_scores, query_tall, 1, 1) * score_scale
        value_part = contract(probs.astype(bf16), grad_tall, 1, 1)
        lane = lax.broadcasted_iota(jnp.int32, key_part.shape, 1)
        both = jnp.where(lane < NOPE, key_part, value_part)
        if start:
            both = both + base[rows, :].astype(f32)
        pair_grad[rows, :] = both.astype(bf16)
        rotary_grad[rows, :] += key_part
        acc[...] += contract(key, grad_scores, 0, 0)

    def skip(block):
        rows = pl.ds(block * span, span)
        if start:
            pair_grad[rows, :] = base[rows, :]
        else:
            pair_grad[rows, :] = jnp.zeros((span, PAIR), bf16)

    for block in range(blocks):
        theirs = places[block]
        pl.when(theirs < mine)(lambda block=block: visit(block, False))
        pl.when(theirs == mine)(lambda block=block: visit(block, True))
        pl.when(theirs > mine)(lambda block=block: skip(block))
    total = acc[...] * score_scale
    former = total[NOPE : NOPE + half, :]
    latter = total[NOPE + half : HEAD, :]
    query_grad[...] = jnp.concatenate(
        [
            total[:NOPE, :],
            former * cosine[...] + latter * sine[...],
            latter * cosine[...] - former * sine[...],
        ],
        axis=0,
    ).astype(bf16)


def attend_back(own, places, query, cosine, sine, pairs, rotary, grad, out, log_total, base):
    rows, tokens = query.shape
    heads = rows // HEAD
    keys = pairs.shape[0]
    span = tokens
    blocks = keys // span
    elements = heads * tokens * keys
    half = ROPE // 2
    start = base is not None

    def kernel(*refs):
        attend_back_kernel(blocks, span, start, own, *refs)

    args = [places, query, cosine, sine, pairs, rotary, grad, out, log_total]
    in_specs = [
        pl.BlockSpec((HEAD, tokens), lambda h, p: (h, 0)),
        pl.BlockSpec((half, tokens), lambda h, p: (0, 0)),
        pl.BlockSpec((half, tokens), lambda h, p: (0, 0)),
        pl.BlockSpec((keys, PAIR), lambda h, p: (0, h)),
        pl.BlockSpec((keys, PAIR), lambda h, p: (0, 0)),
        pl.BlockSpec((VDIM, tokens), lambda h, p: (h, 0)),
        pl.BlockSpec((VDIM, tokens), lambda h, p: (h, 0)),
        pl.BlockSpec((1, 1, tokens), lambda h, p: (h, 0, 0)),
    ]
    if start:
        args.append(base)
        in_specs.append(pl.BlockSpec((keys, PAIR), lambda h, p: (0, h)))
    return pl.pallas_call(
        kernel,
        out_shape=(
            jax.ShapeDtypeStruct((rows, tokens), bf16),
            jax.ShapeDtypeStruct((keys, heads * PAIR), bf16),
            jax.ShapeDtypeStruct((keys, PAIR), f32),
        ),
        grid_spec=pltpu.PrefetchScalarGridSpec(
            num_scalar_prefetch=1,
            grid=(heads,),
            in_specs=in_specs,
            out_specs=(
                pl.BlockSpec((HEAD, tokens), lambda h, p: (h, 0)),
                pl.BlockSpec((keys, PAIR), lambda h, p: (0, h)),
                pl.BlockSpec((keys, PAIR), lambda h, p: (0, 0)),
            ),
            scratch_shapes=[pltpu.VMEM((PAIR, tokens), f32)],
        ),
        compiler_params=pltpu.CompilerParams(vmem_limit_bytes=32 * 1024 * 1024),
        cost_estimate=pl.CostEstimate(
            flops=10 * elements * 128, bytes_accessed=keys * heads * PAIR * 4, transcendentals=elements
        ),
        name="attend_back",
    )(*args)


def ffn_front(normed, grad, weights, tile=256):
    tokens, width = normed.shape
    owners, kinds, rows, units = weights.shape

    def kernel(normed, grad, gate, up, down, hidden, grad_gate, grad_up):
        def product(left, weight):
            weight = weight[...].reshape(width, tile)
            return jnp.dot(left[...], weight, preferred_element_type=f32)

        gate_value = product(normed, gate)
        up_value = product(normed, up)
        grad_hidden = product(grad, down)
        sigma = jax.nn.sigmoid(gate_value)
        silu_gate = gate_value * sigma
        hidden[...] = (silu_gate * up_value).astype(bf16)
        slope = sigma * (1.0 + gate_value * (1.0 - sigma))
        grad_gate[...] = (grad_hidden * up_value * slope).astype(bf16)
        grad_up[...] = (grad_hidden * silu_gate).astype(bf16)

    whole = pl.BlockSpec((tokens, width), lambda n: (0, 0))
    weight = [
        pl.BlockSpec((owners, None, rows, tile), lambda n, kind=kind: (0, kind, 0, n))
        for kind in range(kinds)
    ]
    given = jax.ShapeDtypeStruct((tokens, units), bf16)
    block = pl.BlockSpec((tokens, tile), lambda n: (0, n))
    return pl.pallas_call(
        kernel,
        out_shape=(given, given, given),
        grid=(pl.cdiv(units, tile),),
        in_specs=[whole, whole] + weight,
        out_specs=(block, block, block),
        compiler_params=pltpu.CompilerParams(vmem_limit_bytes=40 * 1024 * 1024),
        cost_estimate=pl.CostEstimate(
            flops=6 * tokens * width * units,
            bytes_accessed=6 * width * units,
            transcendentals=tokens * units,
        ),
        name="ffn_front",
    )(normed, grad, weights, weights, weights)


def owners_at_once(rows):
    step = 1
    while step * rows % 128:
        step += 1
    return step


def rows_product(lefts, weights, kinds):
    tokens, units = lefts[0].shape
    owners, _, rows, _ = weights.shape
    step = owners_at_once(rows)
    tile = step * rows
    width = owners * rows
    count = len(lefts)

    def kernel(*refs):
        total = None
        for i in range(count):
            weight = refs[count + i][...].reshape(tile, units)
            part = contract(refs[i][...], weight, 1, 1)
            total = part if total is None else total + part
        refs[-1][...] = total.astype(bf16)

    whole = pl.BlockSpec((tokens, units), lambda n: (0, 0))
    weight = [
        pl.BlockSpec((step, None, rows, units), lambda n, kind=kind: (n, kind, 0, 0))
        for kind in kinds
    ]
    return pl.pallas_call(
        kernel,
        out_shape=jax.ShapeDtypeStruct((tokens, width), bf16),
        grid=(width // tile,),
        in_specs=[whole] * count + weight,
        out_specs=pl.BlockSpec((tokens, tile), lambda n: (0, n)),
        compiler_params=pltpu.CompilerParams(vmem_limit_bytes=40 * 1024 * 1024),
        cost_estimate=pl.CostEstimate(
            flops=2 * count * tokens * width * units,
            bytes_accessed=2 * count * width * units,
            transcendentals=0,
        ),
        name="rows_product",
    )(*lefts, *([weights] * count))


def weight_grads(groups, owners):
    lefts = []
    for left, _ in groups:
        if not any(left is other for other in lefts):
            lefts.append(left)
    which = [[left is other for other in lefts].index(True) for left, _ in groups]
    parts = len(lefts[0])
    tokens, width = lefts[0][0].shape
    units = groups[0][1][0].shape[1]
    count = len(groups)
    rows = width // owners
    step = owners_at_once(rows)
    tile = step * rows

    def kernel(*refs):
        left = refs[: parts * len(lefts)]
        right = refs[parts * len(lefts) : -1]
        out = refs[-1]
        for g in range(count):
            total = None
            for p in range(parts):
                part = contract(
                    left[which[g] * parts + p][...], right[g * parts + p][...], 0, 0
                )
                total = part if total is None else total + part
            out[:, g] = total.astype(bf16).reshape(step, rows, units)

    left_spec = pl.BlockSpec((tokens, tile), lambda n: (0, n))
    right_spec = pl.BlockSpec(
        (tokens, units), lambda n: (0, 0), pipeline_mode=pl.Buffered(buffer_count=1)
    )
    return pl.pallas_call(
        kernel,
        out_shape=jax.ShapeDtypeStruct((owners, count, rows, units), bf16),
        grid=(width // tile,),
        in_specs=[left_spec] * (parts * len(lefts)) + [right_spec] * (parts * count),
        out_specs=pl.BlockSpec((step, count, rows, units), lambda n: (n, 0, 0, 0)),
        compiler_params=pltpu.CompilerParams(vmem_limit_bytes=44 * 1024 * 1024),
        cost_estimate=pl.CostEstimate(
            flops=2 * parts * count * tokens * width * units,
            bytes_accessed=2 * (parts * count * tokens + count * width) * units,
            transcendentals=0,
        ),
        name="weight_grads",
    )(*[part for left in lefts for part in left], *[part for _, right in groups for part in right])


def pack_ups(output, query, latent):
    lanes = output.shape[1]
    rest = query[:, lanes:]
    rest = jnp.pad(rest, ((0, 0), (0, lanes - rest.shape[1])))
    return jnp.concatenate(
        [output, query[:, :lanes], rest, latent[:, :lanes], latent[:, lanes:]], axis=0
    )


def unpack_ups(packed, output_shape, query_shape, latent_shape):
    lanes = output_shape[1]
    at = output_shape[0]
    query_rows, latent_rows = query_shape[0], latent_shape[0]
    output = packed[..., :at, :]
    query = jnp.concatenate(
        [
            packed[..., at : at + query_rows, :],
            packed[..., at + query_rows : at + 2 * query_rows, : query_shape[1] - lanes],
        ],
        axis=-1,
    )
    at += 2 * query_rows
    latent = jnp.concatenate(
        [packed[..., at : at + latent_rows, :], packed[..., at + latent_rows :, :]], axis=-1
    )
    return output, query, latent


def ups_grads(grad_attn, attended, query_normed, query_grads, latent, pair_grad, owners):
    parts = len(grad_attn)
    tokens, width = grad_attn[0].shape
    lanes = attended[0].shape[0]
    rows, query_rows, latent_rows = (
        size // owners for size in (width, query_normed.shape[0], latent.shape[0])
    )
    columns = query_grads[0].shape[0]
    step = owners_at_once(rows)
    all_rows = rows + 2 * query_rows + 2 * latent_rows
    keys = latent.shape[1]

    def kernel(*refs):
        grads, refs = refs[:parts], refs[parts:]
        outs, refs = refs[:parts], refs[parts:]
        normed, refs = refs[0], refs[1:]
        queries, refs = refs[:parts], refs[parts:]
        latent, pairs, out = refs
        total, query = None, None
        for i in range(parts):
            part = contract(grads[i][...], outs[i][...], 0, 1)
            total = part if total is None else total + part
            part = contract(normed[:, i * tokens : (i + 1) * tokens], queries[i][...], 1, 1)
            query = part if query is None else query + part
        out[:, :rows, :] = total.astype(bf16).reshape(step, rows, lanes)
        query = query.astype(bf16).reshape(step, query_rows, columns)
        at = rows
        out[:, at : at + query_rows, :] = query[:, :, :lanes]
        at += query_rows
        out[:, at : at + query_rows, : columns - lanes] = query[:, :, lanes:]
        out[:, at : at + query_rows, columns - lanes :] = jnp.zeros(
            (step, query_rows, 2 * lanes - columns), bf16
        )
        at += query_rows
        both = jnp.dot(latent[...], pairs[...], preferred_element_type=f32)
        both = both.astype(bf16).reshape(step, latent_rows, 2 * lanes)
        out[:, at : at + latent_rows, :] = both[:, :, :lanes]
        at += latent_rows
        out[:, at : at + latent_rows, :] = both[:, :, lanes:]

    def fixed(shape):
        return pl.BlockSpec(shape, lambda n: (0, 0))

    return pl.pallas_call(
        kernel,
        out_shape=jax.ShapeDtypeStruct((owners, all_rows, lanes), bf16),
        grid=(owners // step,),
        in_specs=[pl.BlockSpec((tokens, step * rows), lambda n: (0, n))] * parts
        + [fixed((lanes, tokens))] * parts
        + [pl.BlockSpec((step * query_rows, parts * tokens), lambda n: (n, 0))]
        + [fixed((columns, tokens))] * parts
        + [pl.BlockSpec((step * latent_rows, keys), lambda n: (n, 0)), fixed(pair_grad.shape)],
        out_specs=pl.BlockSpec((step, all_rows, lanes), lambda n: (n, 0, 0)),
        compiler_params=pltpu.CompilerParams(vmem_limit_bytes=40 * 1024 * 1024),
        cost_estimate=pl.CostEstimate(
            flops=2 * parts * tokens * (width * lanes + query_normed.shape[0] * columns)
            + 4 * keys * latent.shape[0] * lanes,
            bytes_accessed=2 * (owners * all_rows * lanes + keys * lanes * 2),
            transcendentals=0,
        ),
        name="ups_grads",
    )(*grad_attn, *attended, query_normed, *query_grads, latent, pair_grad)


def held(*values):
    out = lax.optimization_barrier(values)
    return out if len(values) > 1 else out[0]


class Order:
    def __init__(self):
        self.last = None

    def take(self, *values):
        if self.last is not None:
            values = lax.optimization_barrier((*values, self.last))[:-1]
        return values if len(values) > 1 else values[0]

    def mark(self, value):
        self.last = value
        return value


def low_sum_of(left, right):
    return (left.astype(f32) + right.astype(f32)).astype(bf16)


class LinePipe:
    def __init__(self, order):
        self.order = order
        self.direct = lax.axis_size("tensor") != 4
        index = lax.axis_index("tensor")
        self.inner = (index == 1) | (index == 2)
        self.waiting = []
        self.entered = None
        self.crossed = None
        self.left = None
        self.sums = {}
        self.count = 0

    def push(self, part, pieces, ahead=False):
        rows = part.shape[0] // pieces
        keys = []
        fresh = []
        for i in range(pieces):
            piece = part[i * rows : (i + 1) * rows]
            keys.append(self.count)
            if self.direct:
                total = lax.psum(piece, "tensor")
                self.sums[self.count] = (total, total)
            else:
                fresh.append((self.count, piece))
            self.count += 1
        self.waiting = fresh + self.waiting if ahead else self.waiting + fresh
        return keys

    def step(self, *others):
        if self.direct:
            return others if len(others) != 1 else others[0]
        arrived = []
        if self.entered is not None:
            arrived += [self.entered[1], self.entered[2]]
        if self.crossed is not None:
            arrived += [self.crossed[1], self.crossed[2]]
        fresh = self.waiting.pop(0) if self.waiting else None
        if fresh is not None:
            arrived.append(fresh[1])
        if self.left is not None:
            others = others + (self.left,)
        if not arrived and not others:
            return None
        taken = self.order.take(*arrived, *others)
        if len(arrived) + len(others) == 1:
            taken = (taken,)
        taken = list(taken)
        if self.left is not None:
            taken.pop()
        half = whole = None
        if self.entered is not None:
            half = low_sum_of(taken.pop(0), taken.pop(0))
        if self.crossed is not None:
            whole = low_sum_of(taken.pop(0), taken.pop(0))
        low = taken.pop(0) if fresh is not None else None
        joint = whole is not None and low is not None and whole.shape == low.shape
        if joint:
            whole, low = None, jnp.where(self.inner, whole, low)
        sends = [value for value in (half, whole, low) if value is not None]
        if sends:
            sends = list(lax.optimization_barrier(tuple(sends)))
            self.order.mark(sends[-1])
        half = sends.pop(0) if half is not None else None
        whole = sends.pop(0) if whole is not None else None
        low = sends.pop(0) if low is not None else None
        crossed, entered, left = None, None, None
        inwards, outwards = [(0, 1), (3, 2)], [(1, 0), (2, 3)]
        if joint:
            got = lax.ppermute(low, "tensor", inwards + outwards)
            self.sums[self.crossed[0]] = (low, got)
            entered = (fresh[0], fresh[1], got)
        elif whole is not None:
            got = left = lax.ppermute(whole, "tensor", outwards)
            self.sums[self.crossed[0]] = (whole, got)
        if low is not None and not joint:
            entered = (fresh[0], low, lax.ppermute(low, "tensor", inwards))
        if half is not None:
            crossed = (self.entered[0], half, lax.ppermute(half, "tensor", [(1, 2), (2, 1)]))
        self.entered, self.crossed, self.left = entered, crossed, left
        return taken if len(taken) != 1 else taken[0]

    def arrived(self):
        got = [] if self.left is None else [self.left]
        return got + [stage[2] for stage in (self.entered, self.crossed) if stage is not None]

    def done(self, keys):
        pieces = [jnp.where(self.inner, *self.sums[key]) for key in keys]
        return jnp.concatenate(pieces, axis=0)


def direct_sum(order, part):
    count = lax.axis_size("tensor")
    if count != 4:
        total = lax.psum(part, "tensor")
        return lambda: total
    index = lax.axis_index("tensor")
    rows = part.shape[0] // count

    def share(k):
        return lax.dynamic_slice_in_dim(part, (index + k) % count * rows, rows, 0)

    shares = held(*[share(k) for k in range(count)])
    order.mark(shares[1])
    got = [
        lax.ppermute(shares[k], "tensor", [(i, (i + k) % count) for i in range(count)])
        for k in (2, 1, 3)
    ]

    def finish():
        mine = order.take(shares[0], *got)
        mine = sum(value.astype(f32) for value in mine).astype(bf16)
        mine = order.mark(held(mine))
        pieces = [mine] + [
            lax.ppermute(mine, "tensor", [((i + k) % count, i) for i in range(count)])
            for k in range(1, count)
        ]
        twice = jnp.concatenate(pieces + pieces, axis=0)
        start = (count - index) % count * rows
        return lax.dynamic_slice_in_dim(twice, start, count * rows, 0)

    return finish


def from_others(rows):
    count = lax.axis_size("ctx")
    return [
        lax.ppermute(rows, "ctx", [((i + k) % count, i) for i in range(count)])
        for k in range(1, count)
    ]


def back_to_owners(blocks):
    count = lax.axis_size("ctx")
    total = blocks[0].astype(f32)
    for k in range(1, count):
        total = total + lax.ppermute(
            blocks[k], "ctx", [(i, (i + k) % count) for i in range(count)]
        ).astype(f32)
    return total


def per_device(
    layer_input,
    cotangent,
    span_order,
    query_down,
    latent_down,
    query_up,
    latent_up,
    output_weight,
    gate_weight,
    up_weight,
    down_weight,
    first_gain,
    query_gain,
    latent_gain,
    second_gain,
):
    ctx_count = lax.axis_size("ctx")
    tensor_count = lax.axis_size("tensor")
    ctx_index = lax.axis_index("ctx")
    part_index = lax.axis_index("tensor")
    tokens = layer_input.shape[1]
    spans = span_order.shape[0] // ctx_count
    span = tokens // spans
    width = layer_input.shape[2]
    chunks = [slice(i * span, (i + 1) * span) for i in range(spans)]
    weights_at = ("dp", "ctx")
    order = Order()

    owners = weights_count()
    down_both = lax.all_gather(
        jnp.concatenate([query_down, latent_down], axis=1), weights_at, axis=0, tiled=True
    )
    inputs = layer_input[0]
    normed_one, factor_one = rms_norm(inputs.astype(f32), first_gain, -1)
    norm_one = normed_one.astype(bf16)
    output_rows = output_weight.T
    shapes = [output_rows.shape, query_up.shape, latent_up.shape]
    ups = pack_ups(output_rows, query_up, latent_up)
    ups, norm_one = held(ups, norm_one)
    ups = lax.all_gather(ups, weights_at, axis=0)

    places = lax.dynamic_slice_in_dim(
        jnp.concatenate([span_order, span_order]), ctx_index * spans, spans * ctx_count
    )
    local_places = (
        places[:spans, None] * span + jnp.arange(span, dtype=jnp.int32)[None, :]
    ).reshape(-1)
    cosine, sine = angles(local_places, ROPE)

    lowered = contract(down_both, norm_one, 0, 1)
    ffn_weights = jnp.stack([gate_weight, up_weight, down_weight.T])
    ffn_weights, lowered = held(ffn_weights, lowered)
    ffn_weights = lax.all_gather(ffn_weights, weights_at, axis=0)
    query_latent = lowered[:QRANK]
    latent_raw = lowered[QRANK : QRANK + KVRANK]
    latent_normed, latent_factor = rms_norm(latent_raw, latent_gain)
    rotary_key = rotate(lowered[QRANK + KVRANK :], cosine, sine)
    latent_pack = jnp.concatenate([latent_normed, rotary_key], axis=0).astype(bf16)
    ups, _ = held(ups, latent_pack)
    sequence_pack = jnp.concatenate([latent_pack] + from_others(latent_pack), axis=1)
    output_all, query_up_all, latent_up_all = [
        part.reshape(-1, part.shape[-1]) for part in unpack_ups(ups, *shapes)
    ]
    query_normed, query_factor = rms_norm(query_latent, query_gain)
    query_normed = query_normed.astype(bf16)
    query_raw = contract(query_up_all, query_normed, 0, 0)
    sequence_latent = sequence_pack[:KVRANK]
    pairs = contract(sequence_latent, latent_up_all, 0, 0).astype(bf16)
    rotary = jnp.pad(sequence_pack[KVRANK:].T, ((0, 0), (NOPE, PAIR - HEAD)))

    grad_ffn = (depth_scale * cotangent[0].astype(f32)).astype(bf16)
    pipe = LinePipe(order)
    attended, queries, log_totals = [], [], []
    attn_sums = []
    for i, rows in enumerate(chunks):
        raw = order.take(query_raw[:, rows])
        out, query, log_total = attend(
            i, places, raw, cosine[:, rows], sine[:, rows], pairs, rotary
        )
        order.mark(out)
        attended.append(out)
        queries.append(query)
        log_totals.append(log_total)
        if i > 0:
            pipe.step()
        part = contract(order.take(out), output_all, 0, 1).astype(bf16)
        attn_sums.append(pipe.push(order.mark(held(part)), 2))
        pipe.step()
    pipe.step()

    def ffn_start(i, rows):
        total = order.take(pipe.done(attn_sums[i]))
        middle = inputs[rows].astype(f32) + depth_scale * total.astype(f32)
        normed_two, factor = rms_norm(middle, second_gain, -1)
        norm_two = order.mark(held(normed_two.astype(bf16)))
        hidden, grad_gate, grad_up = ffn_front(norm_two, grad_ffn[rows], ffn_weights)
        order.mark(hidden)
        return middle, factor, norm_two, hidden, grad_gate, grad_up

    def ffn_end(parts):
        grad_gate, grad_up = order.take(parts[4], parts[5])
        part = rows_product([grad_gate, grad_up], ffn_weights, [0, 1])
        return pipe.push(order.mark(part), 2)

    def reduced(grad):
        return lax.psum_scatter(grad, weights_at, scatter_dimension=0, tiled=grad.ndim == 2)

    def ffn_out(i):
        part = rows_product([order.take(hidden[i])], ffn_weights, [2])
        return order.mark(part)

    mine = ffn_start(0, chunks[0])
    hidden = [mine[3]]
    pipe.step()
    norm_sums = [ffn_end(mine)]
    pipe.step()
    ffn_parts = [ffn_out(0)]
    pipe.step()
    theirs = ffn_start(1, chunks[1])
    pipe.step()
    norm_sums.append(ffn_end(theirs))
    pipe.step()
    middle, factor_two, norm_two, hidden, grad_gate, grad_up = zip(mine, theirs)
    ffn_cots = [order.take(grad_ffn[rows]) for rows in chunks]
    ffn_grads = weight_grads(
        [(norm_two, grad_gate), (norm_two, grad_up), (ffn_cots, hidden)], owners
    )
    order.mark(ffn_grads)
    pipe.step()
    ffn_done = reduced(order.take(ffn_grads))
    ffn_sums = [pipe.push(ffn_parts[0], 2)]

    grad_middle, grad_attn, second_parts = [], [], []
    query_grads, pair_grad, rotary_grad = [], None, 0.0
    for i, rows in enumerate(chunks):
        total = order.take(pipe.done(norm_sums[i]))
        middle_part, second_part = rms_back(
            total.astype(f32), middle[i], factor_two[i], second_gain, -1
        )
        second_parts.append(second_part)
        grad_middle.append(cotangent[0, rows].astype(f32) + middle_part)
        grad_attn.append(held((depth_scale * grad_middle[i]).astype(bf16)))
        order.mark(grad_attn[i])
        grad_attended = contract(output_all, grad_attn[i], 0, 1).astype(bf16)
        query_grad, pair_grad, rotary_part = attend_back(
            i,
            places,
            queries[i],
            cosine[:, rows],
            sine[:, rows],
            pairs,
            rotary,
            grad_attended,
            attended[i],
            log_totals[i],
            pair_grad,
        )
        order.mark(query_grad)
        query_grads.append(query_grad)
        rotary_grad = rotary_grad + rotary_part[:, NOPE:HEAD]
        if i == 0:
            pipe.step()
            ffn_parts.append(ffn_out(1))
            ffn_sums.append(pipe.push(ffn_parts[1], 2))
            pipe.step()
            pipe.step()
    second_gain_grad = sum(second_parts)

    pack_grad = jnp.concatenate(
        [contract(latent_up_all, pair_grad, 1, 1), rotary_grad.T], axis=0
    ).astype(bf16)
    pack_local = back_to_owners(
        [pack_grad[:, k * tokens : (k + 1) * tokens] for k in range(ctx_count)]
    )
    query_part = contract(query_up_all, jnp.concatenate(query_grads, axis=1), 1, 0)
    query_part = order.mark(held(query_part.astype(bf16)))
    outs_grad = ups_grads(
        [order.take(part) for part in grad_attn],
        attended,
        query_normed,
        query_grads,
        sequence_latent,
        pair_grad,
        owners,
    )
    order.mark(outs_grad)
    pack_local = order.take(pack_local, order.last, *pipe.arrived())[0].astype(bf16)
    low_part = order.mark(held(jnp.concatenate([query_part, pack_local], axis=0)))
    low_finish = direct_sum(order, low_part)
    outs_done = reduced(order.take(outs_grad))
    low_sums = low_finish()
    ffn_done = pipe.step(ffn_done)
    both = order.take(low_sums).astype(f32)
    grad_query_latent, query_gain_grad = rms_back(
        both[:QRANK], query_latent, query_factor, query_gain
    )
    grad_latent_normed, latent_gain_grad = rms_back(
        both[QRANK : QRANK + KVRANK], latent_raw, latent_factor, latent_gain
    )
    lowered_grad = jnp.concatenate(
        [grad_query_latent, grad_latent_normed, unrotate(both[QRANK + KVRANK :], cosine, sine)],
        axis=0,
    ).astype(bf16)
    lowered_grad = order.mark(held(lowered_grad))
    lowered_grad, outs_done = order.take(lowered_grad, outs_done)
    query_cols = QRANK // tensor_count
    latent_cols = (KVRANK + ROPE) // tensor_count
    cut = jnp.concatenate(
        [
            lax.dynamic_slice_in_dim(lowered_grad, part_index * query_cols, query_cols, 0),
            lax.dynamic_slice_in_dim(
                lowered_grad, QRANK + part_index * latent_cols, latent_cols, 0
            ),
        ],
        axis=0,
    )
    down_cut = contract(norm_one, cut, 0, 1)
    grad_norm_one = order.mark(contract(lowered_grad, down_both, 0, 1))
    pipe.step()
    _, first_gain_grad = rms_back(
        grad_norm_one, inputs.astype(f32), factor_one, first_gain, -1
    )
    gains = jnp.concatenate(
        [query_gain_grad.reshape(owners, -1), latent_gain_grad.reshape(owners, -1)], axis=1
    )
    gains = jnp.pad(gains, ((0, 0), (0, width // owners - gains.shape[1]))).reshape(-1)
    columns = [first_gain_grad[:, None], second_gain_grad[:, None], gains[:, None]]
    last = jnp.concatenate([down_cut] + columns, axis=1).astype(bf16)
    last = order.take(last)
    last_done = reduced(order.mark(last)).astype(f32)
    grad_norm_one = order.take(grad_norm_one)
    input_part, _ = rms_back(grad_norm_one, inputs.astype(f32), factor_one, first_gain, -1)
    input_rows = jnp.concatenate(grad_middle, axis=0) + input_part
    pipe.step()
    pipe.step()
    qd_done = last_done[:, :query_cols]
    ld_done = last_done[:, query_cols : query_cols + latent_cols]
    first_done = last_done[:, query_cols + latent_cols]
    second_done = last_done[:, query_cols + latent_cols + 1]
    gains_done = last_done[:, query_cols + latent_cols + 2]
    query_done = gains_done[: QRANK // owners]
    latent_done = gains_done[QRANK // owners : (QRANK + KVRANK) // owners]
    out_done, qu_done, lu_done = unpack_ups(outs_done.astype(f32), *shapes)
    out_done = out_done.T
    ffn_done = ffn_done.astype(f32)

    block_rows = [
        (middle[i] + depth_scale * pipe.done(ffn_sums[i]).astype(f32)).astype(bf16)
        for i in range(spans)
    ]
    return (
        jnp.concatenate(block_rows, axis=0)[None],
        input_rows[None],
        qd_done,
        ld_done,
        qu_done,
        lu_done,
        out_done,
        ffn_done[0],
        ffn_done[1],
        ffn_done[2].T,
        first_done,
        query_done,
        latent_done,
        second_done,
    )


def weights_count():
    return lax.axis_size("dp") * lax.axis_size("ctx")


def solution(mesh):
    placed = (
        P("dp", "ctx", None),
        P("dp", "ctx", None),
        P(),
        P(("dp", "ctx"), None),
        P(("dp", "ctx"), None),
        P(("dp", "ctx"), "tensor"),
        P(("dp", "ctx"), "tensor"),
        P("tensor", ("dp", "ctx")),
        P(("dp", "ctx"), "tensor"),
        P(("dp", "ctx"), "tensor"),
        P("tensor", ("dp", "ctx")),
        P(),
        P(),
        P(),
        P(),
    )
    return jax.shard_map(
        per_device,
        mesh=mesh,
        in_specs=placed,
        out_specs=(
            P("dp", "ctx", None),
            P("dp", "ctx", None),
            P(("dp", "ctx"), "tensor"),
            P(("dp", "ctx"), "tensor"),
            P(("dp", "ctx"), "tensor"),
            P(("dp", "ctx"), "tensor"),
            P("tensor", ("dp", "ctx")),
            P(("dp", "ctx"), "tensor"),
            P(("dp", "ctx"), "tensor"),
            P("tensor", ("dp", "ctx")),
            P(("dp", "ctx")),
            P(("dp", "ctx")),
            P(("dp", "ctx")),
            P(("dp", "ctx")),
        ),
        check_vma=False,
    )
```
